32 devices in a mesh: sec: 8 (over y, x, core), tile: 4 (over z).
Axes of the slice: x: 2, y: 2, z: 4, core: 2. Of those that a mesh axis runs over, the one named last changes fastest.
Arguments:
- image: bfloat16 [8, 4096, 1024], P('sec', 'tile'), as said below
- fwd_offset: int32 [8, 2, 32, 8], P('sec', None, 'tile'), may hold values from -16 to 16
- bwd_offset: int32 [8, 2, 32, 8], P('sec', None, 'tile'), may hold values from -16 to 16
- valid: int32 [8, 32, 8], P('sec', 'tile'), may hold values 0 or 1
Outputs:
- pair_flow: float32 [8, 2, 32, 8], P('sec', None, 'tile')
- mesh_shift: float32 [8, 2, 32, 8], P('sec', None, 'tile')
The draws below stay inside these ranges and needn't reach their ends.
Inputs may be any that keep to these rules, and one draw needn't show every extreme that they name: `image`: pixel intensities of order one.
All inputs are finite; a program needn't handle non-finite values. No bound on the sum of `valid` on one device may be relied on, other than what follows from the above.
Results may differ from the reference program's by a relative error of at most 0.0003.
Values may be sent and summed in bfloat16 or wider, within the bound.
No kernel may reach another device: no remote copies, remote signals or barrier semaphores. Data moves between devices by JAX's collectives and lax.ppermute only.
A program may use at most 128 MiB of HBM per device.

```python
import jax
import jax.numpy as jnp
from jax import lax

PATCH = 128
OFFMAX = 16
ITERS = 3
PC = 8
SECTIONS = 8
PROWS = 32
ROWS = 4096
COLS = 1024


def draw_image(key, part):
    key = jax.random.fold_in(key, 11)
    drift_key = jax.random.fold_in(key, 1)
    base_key = jax.random.fold_in(key, 2)
    noise_key = jax.random.fold_in(key, 3)
    steps_taken = jax.random.randint(drift_key, (SECTIONS, 2), -3, 4)
    drift = jnp.cumsum(steps_taken, axis=0).astype(jnp.int32)
    texture = jax.random.normal(base_key, (ROWS, COLS), jnp.float32)

    def moved(offset):
        return jnp.roll(texture, (offset[0], offset[1]), (0, 1))
    stack = jax.vmap(moved)(drift)
    noise = jax.random.normal(noise_key, (SECTIONS, ROWS, COLS), jnp.float32)
    stack = stack + 0.4 * noise
    return jnp.clip(stack, -6.0, 6.0).astype(jnp.bfloat16)


def with_ends(array, stream_key, least, largest):
    longest = array.shape.index(max(array.shape))
    spots = []
    for shift in (0, 1):
        where = [jax.random.randint(jax.random.fold_in(stream_key, axis), (), 0, length) for axis, length in enumerate(array.shape)]
        where[longest] = (where[longest] + shift) % array.shape[longest]
        spots.append(tuple(where))
    return array.at[spots[0]].set(least).at[spots[1]].set(largest)


def setup_inputs(seed: int = 0) -> dict:
    arg_keys = jax.random.split(jax.random.key(seed), 5)
    image = draw_image(jax.random.fold_in(arg_keys[4], 71), 0)
    fwd_offset = with_ends(jax.random.randint(arg_keys[1], (SECTIONS, 2, PROWS, PC), 0 - OFFMAX, OFFMAX + 1), jax.random.fold_in(arg_keys[1], 1), 0 - OFFMAX, OFFMAX).astype(jnp.int32)
    bwd_offset = with_ends(jax.random.randint(arg_keys[2], (SECTIONS, 2, PROWS, PC), 0 - OFFMAX, OFFMAX + 1), jax.random.fold_in(arg_keys[2], 1), 0 - OFFMAX, OFFMAX).astype(jnp.int32)
    valid = with_ends((jax.random.randint(arg_keys[3], (SECTIONS, PROWS, PC), 0, 4) < 3).astype(jnp.int32), jax.random.fold_in(arg_keys[3], 1), 0, 1)
    return {"image": image, "fwd_offset": fwd_offset, "bwd_offset": bwd_offset, "valid": valid}


def lag_values(size):
    index = jnp.arange(size)
    return (((index + size // 2) % size) - size // 2).astype(jnp.float32)


def centroid(first, second):
    left = first.astype(jnp.float32)
    left = left - jnp.mean(left)
    right = second.astype(jnp.float32)
    right = right - jnp.mean(right)
    spectrum = jnp.conj(jnp.fft.fft2(left)) * jnp.fft.fft2(right)
    corr = jnp.real(jnp.fft.ifft2(spectrum)).astype(jnp.float32)
    power = corr * corr
    total = jnp.sum(power) + PATCH * PATCH * 1e-6
    lags = lag_values(PATCH)
    return jnp.stack([jnp.sum(power * lags[:, None]) / total, jnp.sum(power * lags[None, :]) / total])


def section_flows(operands):
    own, after, fwd, bwd = operands
    tops = jnp.broadcast_to((jnp.arange(PROWS) * PATCH + OFFMAX)[:, None], (PROWS, PC)).astype(jnp.int32).ravel()
    lefts = jnp.broadcast_to((jnp.arange(PC) * PATCH + OFFMAX)[None, :], (PROWS, PC)).astype(jnp.int32).ravel()

    def single(top, left, fy, fx, by, bx):
        first = lax.dynamic_slice(own, (top, left), (PATCH, PATCH))
        second = lax.dynamic_slice(after, (top + fy, left + fx), (PATCH, PATCH))
        forward = centroid(first, second) + jnp.stack([fy, fx]).astype(jnp.float32)
        third = lax.dynamic_slice(after, (top, left), (PATCH, PATCH))
        fourth = lax.dynamic_slice(own, (top + by, left + bx), (PATCH, PATCH))
        backward = centroid(third, fourth) + jnp.stack([by, bx]).astype(jnp.float32)
        return 0.5 * (forward - backward)

    flows = jax.vmap(single)(tops, lefts, fwd[0].ravel(), fwd[1].ravel(), bwd[0].ravel(), bwd[1].ravel())
    return flows.T.reshape(2, PROWS, PC)


def plane_term(shift):
    rows = shift[:, :, 1:, :] - shift[:, :, :-1, :]
    cols = shift[:, :, :, 1:] - shift[:, :, :, :-1]
    zero = jnp.zeros((), shift.dtype)
    term = jnp.pad(-rows, ((0, 0), (0, 0), (1, 0), (0, 0))) + jnp.pad(rows, ((0, 0), (0, 0), (0, 1), (0, 0)))
    term = term + jnp.pad(-cols, ((0, 0), (0, 0), (0, 0), (1, 0))) + jnp.pad(cols, ((0, 0), (0, 0), (0, 0), (0, 1)))
    return term + zero


def reference(image, fwd_offset, bwd_offset, valid):
    padded = jnp.pad(image, ((0, 0), (OFFMAX, OFFMAX), (OFFMAX, OFFMAX)))
    after = jnp.concatenate([padded[1:], jnp.zeros_like(padded[:1])], axis=0)
    flows = lax.map(section_flows, (padded, after, fwd_offset, bwd_offset))
    notlast = (jnp.arange(SECTIONS) < SECTIONS - 1).astype(jnp.float32)
    pair_flow = flows * notlast[:, None, None, None]
    weight = valid.astype(jnp.float32) * notlast[:, None, None]
    sums = jnp.sum(weight[:, None] * pair_flow, axis=(2, 3))
    counts = jnp.sum(weight, axis=(1, 2))
    mean_flow = sums / jnp.maximum(counts, 1.0)[:, None]
    start = jnp.cumsum(mean_flow, axis=0) - mean_flow
    shift = jnp.broadcast_to(start[:, :, None, None], pair_flow.shape).astype(jnp.float32)
    weight4 = weight[:, None]
    for step in range(ITERS):
        spring = weight4 * (shift + pair_flow)
        shift_pad = jnp.pad(shift, ((1, 1), (0, 0), (0, 0), (0, 0)))
        spring_pad = jnp.pad(spring, ((1, 1), (0, 0), (0, 0), (0, 0)))
        weight_pad = jnp.pad(weight4, ((1, 1), (0, 0), (0, 0), (0, 0)))
        between = weight4 * (shift_pad[2:] - shift - pair_flow) - (weight_pad[:-2] * shift - spring_pad[:-2])
        shift = shift + 0.25 * (plane_term(shift) + between)
    return pair_flow, shift
```

```python
import functools

import jax
import jax.numpy as jnp
import ml_dtypes
import numpy as np
from jax import lax
from jax.experimental import pallas as pl
from jax.experimental.pallas import tpu as pltpu
from jax.sharding import PartitionSpec as P

PATCH = 128
HALF = PATCH // 2
OFFMAX = 16
ITERS = 3
LANES = 128
BF = jnp.bfloat16
F32 = jnp.float32


def split_table(table):
    high = table.astype(np.float32).astype(ml_dtypes.bfloat16)
    low = (table - high.astype(np.float64)).astype(np.float32).astype(ml_dtypes.bfloat16)
    return high, low


@functools.cache
def tables():
    place = np.arange(PATCH)
    quarter = np.sin(np.arange(PATCH // 4 + 1) * (2 * np.pi / PATCH))
    sine = np.concatenate([quarter, quarter[-2::-1], -quarter[1:], -quarter[-2:0:-1]])
    cosine = np.roll(sine, -PATCH // 4)
    basis = np.zeros((PATCH, PATCH))
    basis[0] = place % 2 == 0
    basis[HALF] = place % 2 == 1
    for u in range(1, HALF):
        basis[u] = cosine[(u * place) % PATCH]
        basis[HALF + u] = sine[(u * place) % PATCH]
    lag = ((place + HALF) % PATCH) - HALF
    full = (basis * lag) @ basis.T
    form = np.zeros((HALF, PATCH))
    form[1:] = 2 * full[HALF + 1 :]
    form[1:, HALF + 1 :] = 0
    form[0, :HALF] = basis[:HALF, HALF]
    basis_high, basis_low = split_table(basis)
    form_high, form_low = split_table(form)

    def side_by_side(part):
        out = np.zeros((2 * PATCH, 2 * PATCH), ml_dtypes.bfloat16)
        for t in range(2):
            for s in range(2):
                out[t * PATCH : (t + 1) * PATCH, s * PATCH + t * HALF : s * PATCH + (t + 1) * HALF] = (
                    part[s * HALF : (s + 1) * HALF].T
                )
        return out

    def columns(part):
        out = np.zeros((2 * PATCH, PATCH), ml_dtypes.bfloat16)
        for t in range(2):
            for s in range(2):
                out[s * PATCH + t * HALF : s * PATCH + (t + 1) * HALF, t * HALF : (t + 1) * HALF] = (
                    part[:, s * HALF : (s + 1) * HALF].T
                )
        return out

    along = np.stack([side_by_side(basis_high), side_by_side(basis_low)])
    down = np.concatenate(
        [np.concatenate([basis_high, basis_high], 1), np.concatenate([basis_low, basis_low * 0], 1)], 0
    )
    form_rows = np.concatenate(
        [np.concatenate([form_high, form_high], 1), np.concatenate([form_low, form_low * 0], 1)], 0
    )
    form_cols = np.concatenate([columns(form_high), columns(form_low)], 1)
    return along, down, form_rows, form_cols


def dot(a, b):
    return jnp.dot(a, b, preferred_element_type=F32)


def split(x):
    high = x.astype(BF)
    return high, (x - high.astype(F32)).astype(BF)


def fill_padded(padded, image_ref, low_ref, high_ref):
    rows, cols = image_ref.shape
    padded[:, 0:LANES] = jnp.zeros((padded.shape[0], LANES), F32)
    padded[:, LANES + cols :] = jnp.zeros((padded.shape[0], LANES), F32)
    padded[2 * OFFMAX + rows :, :] = jnp.zeros((8, padded.shape[1]), F32)
    padded[0:OFFMAX, LANES : LANES + cols] = low_ref[...].astype(F32)
    padded[OFFMAX + rows : 2 * OFFMAX + rows, LANES : LANES + cols] = high_ref[...].astype(F32)

    def step(i, carry):
        r = pl.multiple_of(i * 64, 64)
        padded[pl.ds(r + OFFMAX, 64), LANES : LANES + cols] = image_ref[pl.ds(r, 64), :].astype(F32)
        return carry

    lax.fori_loop(0, rows // 64, step, 0)


def fill_windows(window, padded, off_ref, s, c, rows):
    lane = lax.broadcasted_iota(jnp.int32, (PATCH + 8, LANES), 1)

    def step(i, carry):
        for t in range(2):
            j = 2 * c + t
            oy = off_ref[s, 0, i, j]
            ox = off_ref[s, 1, i, j]
            left = (ox < 0).astype(jnp.int32)
            base = pl.multiple_of((j + 1 - left) * LANES, LANES)
            shift = ox + LANES * left
            top = OFFMAX + oy
            aligned = pl.multiple_of(i * PATCH + (top // 8) * 8, 8)
            block = padded[pl.ds(aligned, PATCH + 8), pl.ds(base, 2 * LANES)]
            turn = jnp.bitwise_and(LANES - shift, LANES - 1)
            first = pltpu.roll(block[:, :LANES], turn, 1)
            second = pltpu.roll(block[:, LANES:], turn, 1)
            cut = jnp.where(lane < LANES - shift, first, second)
            cut = pltpu.roll(cut, PATCH + 8 - top % 8, 0)[:PATCH]
            window[pl.ds(pl.multiple_of(i * PATCH, PATCH), PATCH), t * LANES : (t + 1) * LANES] = cut.astype(BF)
        return carry

    lax.fori_loop(0, rows, step, 0)


def transform(block, along_ref, down_ref):
    part = dot(block, along_ref[0]) + dot(block, along_ref[1])
    high, low = split(part)
    both = dot(down_ref[...], jnp.concatenate([high, low], 0))
    return both[:PATCH] + both[PATCH:]


def store_coefficients(out_ref, coef):
    row = lax.broadcasted_iota(jnp.int32, (8, LANES), 0)
    lane = lax.broadcasted_iota(jnp.int32, (8, LANES), 1)
    corner = jnp.logical_and(row == 0, lane % HALF == 0)
    out_ref[...] = coef
    mean = 0.25 * (
        coef[0:8, :LANES] + coef[0:8, LANES:] + coef[HALF : HALF + 8, :LANES] + coef[HALF : HALF + 8, LANES:]
    )
    mean = jnp.where(corner, mean, 0.0)
    for r in (0, HALF):
        for q in (0, LANES):
            out_ref[r : r + 8, q : q + LANES] = coef[r : r + 8, q : q + LANES] - mean


def own_kernel(off_ref, image_ref, low_ref, high_ref, along_ref, down_ref, patch_out, window_out, padded, window):
    s, c = pl.program_id(0), pl.program_id(1)
    rows = image_ref.shape[0] // PATCH

    @pl.when(c == 0)
    def _():
        fill_padded(padded, image_ref, low_ref, high_ref)

    fill_windows(window, padded, off_ref, s, c, rows)
    lanes = pl.ds(pl.multiple_of(c * 2 * LANES, 2 * LANES), 2 * LANES)

    def step(i, carry):
        down = pl.ds(pl.multiple_of(i * PATCH, PATCH), PATCH)
        store_coefficients(patch_out.at[i], transform(image_ref[down, lanes], along_ref, down_ref))
        store_coefficients(window_out.at[i], transform(window[down, :], along_ref, down_ref))
        return carry

    lax.fori_loop(0, rows, step, 0, unroll=2)


def correlate(a_ref, b_ref, coef, pieces, rows_ref, cols_ref):
    lane = lax.broadcasted_iota(jnp.int32, (16, LANES), 1)
    row = lax.broadcasted_iota(jnp.int32, (16, LANES), 0)
    sign_j = jnp.where(lane % HALF == 0, -1.0, 1.0).astype(F32)
    first_row = jnp.where(row == 0, -1.0, 1.0).astype(F32)
    total = jnp.zeros((16, LANES), F32)
    for g in range(HALF // 16):
        top, bottom = slice(16 * g, 16 * g + 16), slice(HALF + 16 * g, HALF + 16 * g + 16)
        acc, acs, asc, ass = a_ref[top, :LANES], a_ref[top, LANES:], a_ref[bottom, :LANES], a_ref[bottom, LANES:]
        bcc, bcs, bsc, bss = b_ref[top, :LANES], b_ref[top, LANES:], b_ref[bottom, :LANES], b_ref[bottom, LANES:]
        acs_j, ass_j = acs * sign_j, ass * sign_j
        cc = acc * bcc + acs * bcs + asc * bsc + ass * bss
        cs = acc * bcs + asc * bss - (acs_j * bcc + ass_j * bsc)
        turned_sc = asc * bcc + ass * bcs
        turned_ss = asc * bcs - ass_j * bcc
        if g == 0:
            turned_sc, turned_ss = turned_sc * first_row, turned_ss * first_row
        sc = acc * bsc + acs * bss - turned_sc
        ss = acc * bss - acs_j * bsc - turned_ss
        total = total + (cc * cc + cs * cs + sc * sc + ss * ss)
        for where, lanes, value in (
            (top, slice(0, LANES), cc),
            (top, slice(LANES, 2 * LANES), cs),
            (bottom, slice(0, LANES), sc),
            (bottom, slice(LANES, 2 * LANES), ss),
        ):
            high, low = split(value)
            coef[where, lanes] = value
            pieces[where, lanes] = high
            pieces[slice(PATCH + where.start, PATCH + where.stop), lanes] = low
    down = dot(rows_ref[...], pieces[...])
    down = down[:HALF] + down[HALF:]
    across = dot(pieces[...], cols_ref[...])
    across = across[:PATCH, :LANES] + across[:PATCH, LANES:] + across[PATCH:, :LANES]
    row8 = lax.broadcasted_iota(jnp.int32, (8, 2 * LANES), 0)
    head = down[0:8]
    moment_r = jnp.where(row8 == 0, -float(HALF) * head, coef[HALF : HALF + 8, :]) * head
    for g in range(1, HALF // 8):
        moment_r = moment_r + down[8 * g : 8 * g + 8] * coef[HALF + 8 * g : HALF + 8 * g + 8, :]
    moment_r = moment_r[:, :LANES] + moment_r[:, LANES:]
    lane8 = lax.broadcasted_iota(jnp.int32, (8, LANES), 1) % HALF == 0
    moment_c = jnp.zeros((8, LANES), F32)
    for g in range(PATCH // 8):
        piece = across[8 * g : 8 * g + 8]
        other = jnp.where(lane8, -float(HALF) * piece, coef[8 * g : 8 * g + 8, LANES:])
        moment_c = moment_c + other * piece
    add = lambda x: jnp.sum(x, axis=0, keepdims=True)
    return add(total), add(moment_r), add(moment_c)


def pair_kernel(
    place_ref, off_ref, image_ref, low_ref, high_ref, along_ref, down_ref, rows_ref, cols_ref,
    own_patch, own_window, fwd_ref, bwd_ref, valid_ref, flow_out, tile_out,
    padded, window, left, right, coef, pieces, sums,
):
    s, c = pl.program_id(0), pl.program_id(1)
    rows = image_ref.shape[0] // PATCH
    pairs = pl.num_programs(1)

    @pl.when(c == 0)
    def _():
        fill_padded(padded, image_ref, low_ref, high_ref)

    fill_windows(window, padded, off_ref, s, c, rows)
    lanes = pl.ds(pl.multiple_of(c * 2 * LANES, 2 * LANES), 2 * LANES)

    def step(i, carry):
        down = pl.ds(pl.multiple_of(i * PATCH, PATCH), PATCH)
        store_coefficients(left, transform(image_ref[down, lanes], along_ref, down_ref))
        store_coefficients(right, transform(window[down, :], along_ref, down_ref))
        forward = correlate(own_patch.at[i], right, coef.at[0], pieces.at[0], rows_ref, cols_ref)
        backward = correlate(left, own_window.at[i], coef.at[1], pieces.at[1], rows_ref, cols_ref)
        for k, value in enumerate(forward + backward):
            sums[k, c, pl.ds(i, 1), :] = value
        return carry

    lax.fori_loop(0, rows, step, 0)

    @pl.when(c == pairs - 1)
    def _():
        count = 2 * sums.shape[1]
        lane = lax.broadcasted_iota(jnp.int32, (rows, LANES), 1)
        gathered = []
        for k in range(6):
            value = jnp.zeros((rows, LANES), F32)
            for p in range(sums.shape[1]):
                held = sums[k, p]
                for t in range(2):
                    mine = (lane >= HALF) if t else (lane < HALF)
                    value = jnp.where(
                        lane == 2 * p + t, jnp.sum(jnp.where(mine, held, 0.0), axis=1, keepdims=True), value
                    )
            gathered.append(value[:, :count])
        scale = (2.0 / PATCH) ** 4 * HALF * HALF
        lag_scale = scale / HALF
        eps = PATCH * PATCH * 1e-6
        notlast = place_ref[s].astype(F32)
        weight = valid_ref[...].astype(F32) * notlast
        flows = []
        for comp in range(2):
            fwd = gathered[1 + comp] * lag_scale / (gathered[0] * scale + eps) + fwd_ref[comp].astype(F32)
            bwd = gathered[4 + comp] * lag_scale / (gathered[3] * scale + eps) + bwd_ref[comp].astype(F32)
            flow = 0.5 * (fwd - bwd) * notlast
            flow_out[comp] = flow
            flows.append(flow)
        fill = jnp.zeros((rows, LANES - 4 * count), F32)
        tile_out[...] = jnp.concatenate(flows + [weight, weight, fill], axis=1)


def mesh_kernel(place_ref, all_ref, shift_out, held):
    sections, height, _ = all_ref.shape
    sec_dev, _, rows, count = shift_out.shape
    lane = lax.broadcasted_iota(jnp.int32, (1, height, LANES), 2)
    down = lax.broadcasted_iota(jnp.int32, (1, height, LANES), 1)
    used = lane < 2 * count
    first = lane < count
    everything = all_ref[...]
    flow = jnp.where(used, everything, 0.0)
    weight = jnp.where(used, pltpu.roll(everything, LANES - 2 * count, 2), 0.0)
    pulled = weight * flow
    counts = jnp.sum(jnp.sum(jnp.where(first, weight, 0.0), axis=1, keepdims=True), axis=2, keepdims=True)
    weighted = jnp.sum(pulled, axis=1, keepdims=True)
    lane1 = lax.broadcasted_iota(jnp.int32, (1, 1, LANES), 2)
    sum_y = jnp.sum(jnp.where(lane1 < count, weighted, 0.0), axis=2, keepdims=True)
    sum_x = jnp.sum(jnp.where(lane1 >= count, weighted, 0.0), axis=2, keepdims=True)
    many = jnp.maximum(counts, 1.0)
    mean = jnp.where(first, sum_y / many, sum_x / many)
    starts = []
    start = jnp.zeros((1, height, LANES), F32)
    for k in range(sections):
        starts.append(start)
        start = start + mean[k : k + 1]
    shift = jnp.concatenate(starts, 0)
    zero = jnp.zeros((1, height, LANES), F32)
    col = lane % count
    has_left, has_right = (col > 0).astype(F32), (col < count - 1).astype(F32)
    has_up, has_down = (down > 0).astype(F32), (down < height - 1).astype(F32)
    degree = has_left + has_right + has_up + has_down
    for _ in range(ITERS):
        plane = (
            has_up * pltpu.roll(shift, 1, 1)
            + has_down * pltpu.roll(shift, height - 1, 1)
            + has_left * pltpu.roll(shift, 1, 2)
            + has_right * pltpu.roll(shift, LANES - 1, 2)
            - degree * shift
        )
        after = jnp.concatenate([shift[1:], zero], 0)
        spring = weight * (after - shift) - pulled
        between = spring - jnp.concatenate([zero, spring[:-1]], 0)
        shift = shift + 0.25 * (plane + between)
    held[...] = shift
    for k in range(sec_dev):
        mine = held[place_ref[0] + k, pl.ds(pl.multiple_of(place_ref[1], 8), rows), :]
        shift_out[k, 0] = mine[:, :count]
        shift_out[k, 1] = mine[:, count : 2 * count]


def section_spec(shape):
    return pl.BlockSpec((None,) + shape[1:], lambda s, c: (s,) + (0,) * (len(shape) - 1))


def whole_spec(shape):
    return pl.BlockSpec(shape, lambda s, c: (0,) * len(shape))


SCALARS = pl.BlockSpec(memory_space=pltpu.SMEM)


def body(image, fwd_offset, bwd_offset, valid):
    sec_dev, height, width = image.shape
    rows, count = valid.shape[1:]
    pairs = count // 2
    sec_size, tile_size = lax.axis_size("sec"), lax.axis_size("tile")
    sections = sec_dev * sec_size
    along, down, form_rows, form_cols = (jnp.asarray(t) for t in tables())

    earlier = [(i, i - 1) for i in range(1, sec_size)]
    arriving = lax.ppermute(image[:1], "sec", earlier)
    up = [(i, i + 1) for i in range(tile_size - 1)]
    back = [(i + 1, i) for i in range(tile_size - 1)]
    low = lax.ppermute(image[:, -OFFMAX:], "tile", up)
    high = lax.ppermute(image[:, :OFFMAX], "tile", back)
    edges = lax.ppermute(jnp.concatenate([low[:1], high[:1]], 1), "sec", earlier)
    after = jnp.concatenate([image[1:], arriving], 0)
    after_low = jnp.concatenate([low[1:], edges[:, :OFFMAX]], 0)
    after_high = jnp.concatenate([high[1:], edges[:, OFFMAX:]], 0)

    coef_shape = jax.ShapeDtypeStruct((sec_dev, pairs, rows, PATCH, 2 * PATCH), F32)
    coef_spec = pl.BlockSpec((None, None, rows, PATCH, 2 * PATCH), lambda s, c: (s, c, 0, 0, 0))
    padded = pltpu.VMEM((height + 2 * OFFMAX + 8, width + 2 * LANES), F32)
    window = pltpu.VMEM((height, 2 * LANES), BF)
    own_patch, own_window = pl.pallas_call(
        own_kernel,
        grid=(sec_dev, pairs),
        out_shape=(coef_shape, coef_shape),
        in_specs=[
            SCALARS,
            section_spec(image.shape),
            section_spec(low.shape),
            section_spec(high.shape),
            whole_spec(along.shape),
            whole_spec(down.shape),
        ],
        out_specs=(coef_spec, coef_spec),
        scratch_shapes=[padded, window],
        compiler_params=pltpu.CompilerParams(vmem_limit_bytes=48 * 1024 * 1024),
        cost_estimate=pl.CostEstimate(flops=10**10, bytes_accessed=10**7, transcendentals=0),
        name="own_spectra",
    )(bwd_offset, image, low, high, along, down)

    place = lax.axis_index("sec") * sec_dev
    notlast = (place + jnp.arange(sec_dev, dtype=jnp.int32) < sections - 1).astype(jnp.int32)
    flow_shape = jax.ShapeDtypeStruct((sec_dev, 2, rows, count), F32)
    pair_flow, tile = pl.pallas_call(
        pair_kernel,
        grid=(sec_dev, pairs),
        out_shape=(flow_shape, jax.ShapeDtypeStruct((sec_dev, rows, LANES), F32)),
        in_specs=[
            SCALARS,
            SCALARS,
            section_spec(after.shape),
            section_spec(after_low.shape),
            section_spec(after_high.shape),
            whole_spec(along.shape),
            whole_spec(down.shape),
            whole_spec(form_rows.shape),
            whole_spec(form_cols.shape),
            coef_spec,
            coef_spec,
            section_spec(fwd_offset.shape),
            section_spec(bwd_offset.shape),
            section_spec(valid.shape),
        ],
        out_specs=(section_spec(flow_shape.shape), section_spec((sec_dev, rows, LANES))),
        scratch_shapes=[
            padded,
            window,
            pltpu.VMEM((PATCH, 2 * PATCH), F32),
            pltpu.VMEM((PATCH, 2 * PATCH), F32),
            pltpu.VMEM((2, PATCH, 2 * PATCH), F32),
            pltpu.VMEM((2, 2 * PATCH, 2 * PATCH), BF),
            pltpu.VMEM((6, pairs, rows, LANES), F32),
        ],
        compiler_params=pltpu.CompilerParams(vmem_limit_bytes=48 * 1024 * 1024),
        cost_estimate=pl.CostEstimate(flops=10**10, bytes_accessed=10**7, transcendentals=0),
        name="pair_flows",
    )(notlast, fwd_offset, after, after_low, after_high, along, down, form_rows, form_cols,
      own_patch, own_window, fwd_offset, bwd_offset, valid)

    devices = sec_size * tile_size
    everywhere = lax.all_to_all(jnp.broadcast_to(tile[None], (devices,) + tile.shape), ("sec", "tile"), 0, 0)
    everywhere = (
        everywhere.reshape(sec_size, tile_size, sec_dev, rows, LANES)
        .transpose(0, 2, 1, 3, 4)
        .reshape(sections, tile_size * rows, LANES)
    )
    where = jnp.stack([place, lax.axis_index("tile") * rows]).astype(jnp.int32)
    mesh_shift = pl.pallas_call(
        mesh_kernel,
        out_shape=flow_shape,
        in_specs=[SCALARS, pl.BlockSpec(memory_space=pltpu.VMEM)],
        out_specs=pl.BlockSpec(memory_space=pltpu.VMEM),
        scratch_shapes=[pltpu.VMEM((sections, tile_size * rows, LANES), F32)],
        name="relax",
    )(where, everywhere)
    return pair_flow, mesh_shift


def solution(mesh):
    return jax.shard_map(
        body,
        mesh=mesh,
        in_specs=(
            P("sec", "tile", None),
            P("sec", None, "tile", None),
            P("sec", None, "tile", None),
            P("sec", "tile", None),
        ),
        out_specs=(P("sec", None, "tile", None), P("sec", None, "tile", None)),
        check_vma=False,
    )
```

```python
import functools

import jax
import jax.numpy as jnp
import ml_dtypes
import numpy as np
from jax import lax
from jax.experimental import pallas as pl
from jax.experimental.pallas import tpu as pltpu
from jax.sharding import PartitionSpec as P

PATCH = 128
HALF = PATCH // 2
OFFMAX = 16
ITERS = 3
LANES = 128
BF = jnp.bfloat16
F32 = jnp.float32


def split_table(table):
    high = table.astype(np.float32).astype(ml_dtypes.bfloat16)
    low = (table - high.astype(np.float64)).astype(np.float32).astype(ml_dtypes.bfloat16)
    return high, low


@functools.cache
def tables():
    place = np.arange(PATCH)
    quarter = np.sin(np.arange(PATCH // 4 + 1) * (2 * np.pi / PATCH))
    sine = np.concatenate([quarter, quarter[-2::-1], -quarter[1:], -quarter[-2:0:-1]])
    cosine = np.roll(sine, -PATCH // 4)
    basis = np.zeros((PATCH, PATCH))
    basis[0] = place % 2 == 0
    basis[HALF] = place % 2 == 1
    for u in range(1, HALF):
        basis[u] = cosine[(u * place) % PATCH]
        basis[HALF + u] = sine[(u * place) % PATCH]
    lag = ((place + HALF) % PATCH) - HALF
    full = (basis * lag) @ basis.T
    form = np.zeros((HALF, PATCH))
    form[1:] = 2 * full[HALF + 1 :]
    form[1:, HALF + 1 :] = 0
    form[0, :HALF] = basis[:HALF, HALF]
    basis_high, basis_low = split_table(basis)
    form_high, form_low = split_table(form)

    def side_by_side(part):
        out = np.zeros((2 * PATCH, 2 * PATCH), ml_dtypes.bfloat16)
        for t in range(2):
            for s in range(2):
                out[t * PATCH : (t + 1) * PATCH, s * PATCH + t * HALF : s * PATCH + (t + 1) * HALF] = (
                    part[s * HALF : (s + 1) * HALF].T
                )
        return out

    def columns(part):
        out = np.zeros((2 * PATCH, PATCH), ml_dtypes.bfloat16)
        for t in range(2):
            for s in range(2):
                out[s * PATCH + t * HALF : s * PATCH + (t + 1) * HALF, t * HALF : (t + 1) * HALF] = (
                    part[:, s * HALF : (s + 1) * HALF].T
                )
        return out

    along = np.concatenate([side_by_side(basis_high), side_by_side(basis_low)], 0)
    down = np.concatenate(
        [np.concatenate([basis_high, basis_high], 1), np.concatenate([basis_low, basis_low * 0], 1)], 0
    )
    form_rows = np.concatenate(
        [np.concatenate([form_high, form_high], 1), np.concatenate([form_low, form_low * 0], 1)], 0
    )
    form_cols = np.concatenate([columns(form_high), columns(form_low)], 1)
    return along, down, form_rows, form_cols


def dot(a, b):
    return jnp.dot(a, b, preferred_element_type=F32)


def split(x):
    high = x.astype(BF)
    return high, (x - high.astype(F32)).astype(BF)


def fill_padded(padded, image_ref, low_ref, high_ref):
    rows, cols = image_ref.shape
    padded[:, 0:LANES] = jnp.zeros((padded.shape[0], LANES), F32)
    padded[:, LANES + cols :] = jnp.zeros((padded.shape[0], LANES), F32)
    padded[2 * OFFMAX + rows :, :] = jnp.zeros((8, padded.shape[1]), F32)
    padded[0:OFFMAX, LANES : LANES + cols] = low_ref[...].astype(F32)
    padded[OFFMAX + rows : 2 * OFFMAX + rows, LANES : LANES + cols] = high_ref[...].astype(F32)

    def step(i, carry):
        r = pl.multiple_of(i * 64, 64)
        padded[pl.ds(r + OFFMAX, 64), LANES : LANES + cols] = image_ref[pl.ds(r, 64), :].astype(F32)
        return carry

    lax.fori_loop(0, rows // 64, step, 0)


def fill_window_row(window, padded, off_ref, s, c, i):
    lane = lax.broadcasted_iota(jnp.int32, (PATCH + 8, LANES), 1)
    deep = lax.broadcasted_iota(jnp.int32, (PATCH // 8, 8, LANES), 1)
    for t in range(2):
        j = 2 * c + t
        top = OFFMAX + off_ref[s, 0, i, j]
        ox = off_ref[s, 1, i, j]
        left = (ox < 0).astype(jnp.int32)
        base = pl.multiple_of((j + 1 - left) * LANES, LANES)
        shift = ox + LANES * left
        aligned = pl.multiple_of(i * PATCH + jnp.bitwise_and(top, -8), 8)
        block = padded[pl.ds(aligned, PATCH + 8), pl.ds(base, 2 * LANES)]
        turn = jnp.bitwise_and(LANES - shift, LANES - 1)
        first = pltpu.roll(block[:, :LANES], turn, 1)
        second = pltpu.roll(block[:, LANES:], turn, 1)
        cut = jnp.where(lane < LANES - shift, first, second)
        over = jnp.bitwise_and(top, 7)
        cut = pltpu.roll(cut.reshape(PATCH // 8 + 1, 8, LANES), jnp.bitwise_and(8 - over, 7), 1)
        cut = jnp.where(deep < 8 - over, cut[:-1], cut[1:]).reshape(PATCH, LANES)
        window[i * PATCH : (i + 1) * PATCH, t * LANES : (t + 1) * LANES] = cut.astype(BF)


def first_stage(block, along_ref, parts):
    high, low = split(dot(jnp.concatenate([block, block], 1), along_ref[...]))
    rows = parts.shape[0]
    parts[:, :PATCH] = high.reshape(rows, PATCH, 2 * PATCH)
    parts[:, PATCH:] = low.reshape(rows, PATCH, 2 * PATCH)


def second_stage(part, down_ref):
    both = dot(down_ref[...], part)
    return both[:PATCH] + both[PATCH:]


def store_coefficients(out_ref, coef):
    row = lax.broadcasted_iota(jnp.int32, (8, LANES), 0)
    lane = lax.broadcasted_iota(jnp.int32, (8, LANES), 1)
    corner = jnp.logical_and(row == 0, lane % HALF == 0)
    out_ref[...] = coef
    mean = 0.25 * (
        coef[0:8, :LANES] + coef[0:8, LANES:] + coef[HALF : HALF + 8, :LANES] + coef[HALF : HALF + 8, LANES:]
    )
    mean = jnp.where(corner, mean, 0.0)
    for r in (0, HALF):
        for q in (0, LANES):
            out_ref[r : r + 8, q : q + LANES] = coef[r : r + 8, q : q + LANES] - mean


def patch_kernel(image_ref, along_ref, down_ref, out_ref, parts):
    rows = image_ref.shape[0] // PATCH
    s, c = pl.program_id(0), pl.program_id(1)
    first_stage(image_ref[...], along_ref, parts)
    for i in range(rows):
        store_coefficients(out_ref.at[s, c, i], second_stage(parts[i], down_ref))


def window_kernel(off_ref, image_ref, low_ref, high_ref, along_ref, down_ref, out_ref, padded, window, parts):
    s, c = pl.program_id(0), pl.program_id(1)
    rows = image_ref.shape[0] // PATCH

    @pl.when(c == 0)
    def _():
        fill_padded(padded, image_ref, low_ref, high_ref)
        for i in range(rows):
            fill_window_row(window.at[0], padded, off_ref, s, 0, i)

    first_stage(window[c % 2], along_ref, parts)
    following = jnp.minimum(c + 1, pl.num_programs(1) - 1)
    for i in range(rows):
        store_coefficients(out_ref.at[s, c, i], second_stage(parts[i], down_ref))
        fill_window_row(window.at[(c + 1) % 2], padded, off_ref, s, following, i)


def cross(a_ref, b_ref, coef, pieces):
    lane = lax.broadcasted_iota(jnp.int32, (16, LANES), 1)
    row = lax.broadcasted_iota(jnp.int32, (16, LANES), 0)
    sign_j = jnp.where(lane % HALF == 0, -1.0, 1.0).astype(F32)
    first_row = jnp.where(row == 0, -1.0, 1.0).astype(F32)
    total = jnp.zeros((16, LANES), F32)
    for g in range(HALF // 16):
        top, bottom = slice(16 * g, 16 * g + 16), slice(HALF + 16 * g, HALF + 16 * g + 16)
        acc, acs, asc, ass = a_ref[top, :LANES], a_ref[top, LANES:], a_ref[bottom, :LANES], a_ref[bottom, LANES:]
        bcc, bcs, bsc, bss = b_ref[top, :LANES], b_ref[top, LANES:], b_ref[bottom, :LANES], b_ref[bottom, LANES:]
        acs_j, ass_j = acs * sign_j, ass * sign_j
        cc = acc * bcc + acs * bcs + asc * bsc + ass * bss
        cs = acc * bcs + asc * bss - (acs_j * bcc + ass_j * bsc)
        turned_sc = asc * bcc + ass * bcs
        turned_ss = asc * bcs - ass_j * bcc
        if g == 0:
            turned_sc, turned_ss = turned_sc * first_row, turned_ss * first_row
        sc = acc * bsc + acs * bss - turned_sc
        ss = acc * bss - acs_j * bsc - turned_ss
        total = total + (cc * cc + cs * cs + sc * sc + ss * ss)
        for where, lanes, value in (
            (top, slice(0, LANES), cc),
            (top, slice(LANES, 2 * LANES), cs),
            (bottom, slice(0, LANES), sc),
            (bottom, slice(LANES, 2 * LANES), ss),
        ):
            high, low = split(value)
            coef[where, lanes] = value
            pieces[where, lanes] = high
            pieces[slice(PATCH + where.start, PATCH + where.stop), lanes] = low
    return jnp.sum(total, axis=0, keepdims=True)


def moments(coef, pieces, rows_ref, cols_ref):
    down = dot(rows_ref[...], pieces[...])
    across = dot(pieces[...], cols_ref[...])
    down = down[:HALF] + down[HALF:]
    across = across[:PATCH, :LANES] + across[:PATCH, LANES:] + across[PATCH:, :LANES]
    row8 = lax.broadcasted_iota(jnp.int32, (8, 2 * LANES), 0)
    head = down[0:8]
    moment_r = jnp.where(row8 == 0, -float(HALF) * head, coef[HALF : HALF + 8, :]) * head
    for g in range(1, HALF // 8):
        moment_r = moment_r + down[8 * g : 8 * g + 8] * coef[HALF + 8 * g : HALF + 8 * g + 8, :]
    moment_r = moment_r[:, :LANES] + moment_r[:, LANES:]
    lane8 = lax.broadcasted_iota(jnp.int32, (8, LANES), 1) % HALF == 0
    moment_c = jnp.zeros((8, LANES), F32)
    for g in range(PATCH // 8):
        piece = across[8 * g : 8 * g + 8]
        other = jnp.where(lane8, -float(HALF) * piece, coef[8 * g : 8 * g + 8, LANES:])
        moment_c = moment_c + other * piece
    return jnp.sum(moment_r, axis=0, keepdims=True), jnp.sum(moment_c, axis=0, keepdims=True)


def pair_kernel(
    place_ref, off_ref, image_ref, low_ref, high_ref, along_ref, down_ref, rows_ref, cols_ref,
    own_patch, own_window, fwd_ref, bwd_ref, valid_ref, flow_out, tile_out,
    padded, window, parts, left, right, coef, pieces, sums,
):
    s, c = pl.program_id(0), pl.program_id(1)
    rows = image_ref.shape[0] // PATCH
    pairs = pl.num_programs(1)

    @pl.when(c == 0)
    def _():
        fill_padded(padded, image_ref, low_ref, high_ref)
        for i in range(rows):
            fill_window_row(window.at[0], padded, off_ref, s, 0, i)

    lanes = pl.ds(pl.multiple_of(c * 2 * LANES, 2 * LANES), 2 * LANES)
    first_stage(image_ref[:, lanes], along_ref, parts.at[0])
    first_stage(window[c % 2], along_ref, parts.at[1])
    following = jnp.minimum(c + 1, pairs - 1)

    def spectra(i):
        store_coefficients(left.at[i % 2], second_stage(parts[0, i], down_ref))
        store_coefficients(right.at[i % 2], second_stage(parts[1, i], down_ref))

    def products(i):
        k = i % 2
        sums[0, c, i : i + 1, :] = cross(own_patch.at[s, c, i], right.at[k], coef.at[0, k], pieces.at[0, k])
        sums[3, c, i : i + 1, :] = cross(left.at[k], own_window.at[s, c, i], coef.at[1, k], pieces.at[1, k])

    def centroid(i):
        for d in range(2):
            by_row, by_col = moments(coef.at[d, i % 2], pieces.at[d, i % 2], rows_ref, cols_ref)
            sums[3 * d + 1, c, i : i + 1, :] = by_row
            sums[3 * d + 2, c, i : i + 1, :] = by_col

    spectra(0)
    for i in range(rows):
        if i + 1 < rows:
            spectra(i + 1)
        products(i)
        fill_window_row(window.at[(c + 1) % 2], padded, off_ref, s, following, i)
        if i:
            centroid(i - 1)
    centroid(rows - 1)

    @pl.when(c == pairs - 1)
    def _():
        count = 2 * sums.shape[1]
        lane = lax.broadcasted_iota(jnp.int32, (rows, LANES), 1)
        gathered = []
        for k in range(6):
            value = jnp.zeros((rows, LANES), F32)
            for p in range(sums.shape[1]):
                held = sums[k, p]
                for t in range(2):
                    mine = (lane >= HALF) if t else (lane < HALF)
                    value = jnp.where(
                        lane == 2 * p + t, jnp.sum(jnp.where(mine, held, 0.0), axis=1, keepdims=True), value
                    )
            gathered.append(value[:, :count])
        scale = (2.0 / PATCH) ** 4 * HALF * HALF
        lag_scale = scale / HALF
        eps = PATCH * PATCH * 1e-6
        notlast = place_ref[s].astype(F32)
        weight = valid_ref[...].astype(F32) * notlast
        flows = []
        for comp in range(2):
            fwd = gathered[1 + comp] * lag_scale / (gathered[0] * scale + eps) + fwd_ref[comp].astype(F32)
            bwd = gathered[4 + comp] * lag_scale / (gathered[3] * scale + eps) + bwd_ref[comp].astype(F32)
            flow = 0.5 * (fwd - bwd) * notlast
            flow_out[comp] = flow
            flows.append(flow)
        fill = jnp.zeros((rows, LANES - 4 * count), F32)
        tile_out[...] = jnp.concatenate(flows + [weight, weight, fill], axis=1)


def mesh_kernel(place_ref, all_ref, shift_out, held):
    sections, height, _ = all_ref.shape
    sec_dev, _, rows, count = shift_out.shape
    lane = lax.broadcasted_iota(jnp.int32, (1, height, LANES), 2)
    down = lax.broadcasted_iota(jnp.int32, (1, height, LANES), 1)
    used = lane < 2 * count
    first = lane < count
    everything = all_ref[...]
    flow = jnp.where(used, everything, 0.0)
    weight = jnp.where(used, pltpu.roll(everything, LANES - 2 * count, 2), 0.0)
    pulled = weight * flow
    counts = jnp.sum(jnp.sum(jnp.where(first, weight, 0.0), axis=1, keepdims=True), axis=2, keepdims=True)
    weighted = jnp.sum(pulled, axis=1, keepdims=True)
    lane1 = lax.broadcasted_iota(jnp.int32, (1, 1, LANES), 2)
    sum_y = jnp.sum(jnp.where(lane1 < count, weighted, 0.0), axis=2, keepdims=True)
    sum_x = jnp.sum(jnp.where(lane1 >= count, weighted, 0.0), axis=2, keepdims=True)
    many = jnp.maximum(counts, 1.0)
    mean = jnp.where(first, sum_y / many, sum_x / many)
    starts = []
    start = jnp.zeros((1, height, LANES), F32)
    for k in range(sections):
        starts.append(start)
        start = start + mean[k : k + 1]
    shift = jnp.concatenate(starts, 0)
    zero = jnp.zeros((1, height, LANES), F32)
    col = lane % count
    has_left, has_right = (col > 0).astype(F32), (col < count - 1).astype(F32)
    has_up, has_down = (down > 0).astype(F32), (down < height - 1).astype(F32)
    degree = has_left + has_right + has_up + has_down
    for _ in range(ITERS):
        plane = (
            has_up * pltpu.roll(shift, 1, 1)
            + has_down * pltpu.roll(shift, height - 1, 1)
            + has_left * pltpu.roll(shift, 1, 2)
            + has_right * pltpu.roll(shift, LANES - 1, 2)
            - degree * shift
        )
        after = jnp.concatenate([shift[1:], zero], 0)
        spring = weight * (after - shift) - pulled
        between = spring - jnp.concatenate([zero, spring[:-1]], 0)
        shift = shift + 0.25 * (plane + between)
    held[...] = shift
    for k in range(sec_dev):
        mine = held[place_ref[0] + k, pl.ds(pl.multiple_of(place_ref[1], 8), rows), :]
        shift_out[k, 0] = mine[:, :count]
        shift_out[k, 1] = mine[:, count : 2 * count]


def section_spec(shape):
    return pl.BlockSpec((None,) + shape[1:], lambda s, c: (s,) + (0,) * (len(shape) - 1))


def whole_spec(shape):
    return pl.BlockSpec(shape, lambda s, c: (0,) * len(shape))


SCALARS = pl.BlockSpec(memory_space=pltpu.SMEM)


PARAMS = pltpu.CompilerParams(vmem_limit_bytes=24 * 1024 * 1024)


def cost(flops):
    return pl.CostEstimate(flops=flops, bytes_accessed=10**7, transcendentals=0)


def coef_layout(sec_dev, rows, pairs):
    return pltpu.VMEM((sec_dev, pairs, rows, PATCH, 2 * PATCH), F32), pl.BlockSpec(memory_space=pltpu.VMEM)


def patch_spectra(image, rows, pairs):
    sec_dev, height, width = image.shape
    along, down, _, _ = (jnp.asarray(t) for t in tables())
    shape, spec = coef_layout(sec_dev, rows, pairs)
    return pl.pallas_call(
        patch_kernel,
        grid=(sec_dev, pairs),
        out_shape=shape,
        in_specs=[
            pl.BlockSpec((None, height, 2 * LANES), lambda s, c: (s, 0, c)),
            whole_spec(along.shape),
            whole_spec(down.shape),
        ],
        out_specs=spec,
        scratch_shapes=[pltpu.VMEM((rows, 2 * PATCH, 2 * PATCH), BF)],
        compiler_params=PARAMS,
        cost_estimate=cost(5 * 10**9),
        name="patch_spectra",
    )(image, along, down)


def window_spectra(offset, image, low, high, rows, pairs):
    sec_dev, height, width = image.shape
    along, down, _, _ = (jnp.asarray(t) for t in tables())
    shape, spec = coef_layout(sec_dev, rows, pairs)
    return pl.pallas_call(
        window_kernel,
        grid=(sec_dev, pairs),
        out_shape=shape,
        in_specs=[
            SCALARS,
            section_spec(image.shape),
            section_spec(low.shape),
            section_spec(high.shape),
            whole_spec(along.shape),
            whole_spec(down.shape),
        ],
        out_specs=spec,
        scratch_shapes=[
            pltpu.VMEM((height + 2 * OFFMAX + 8, width + 2 * LANES), F32),
            pltpu.VMEM((2, height, 2 * LANES), BF),
            pltpu.VMEM((rows, 2 * PATCH, 2 * PATCH), BF),
        ],
        compiler_params=PARAMS,
        cost_estimate=cost(5 * 10**9),
        name="window_spectra",
    )(offset, image, low, high, along, down)


def pair_flows(notlast, fwd_offset, after, after_low, after_high, own_patch, own_window, bwd_offset, valid):
    sec_dev, height, width = after.shape
    rows, count = valid.shape[1:]
    pairs = count // 2
    along, down, form_rows, form_cols = (jnp.asarray(t) for t in tables())
    _, coef_spec = coef_layout(sec_dev, rows, pairs)
    flow_shape = jax.ShapeDtypeStruct((sec_dev, 2, rows, count), F32)
    return pl.pallas_call(
        pair_kernel,
        grid=(sec_dev, pairs),
        out_shape=(flow_shape, jax.ShapeDtypeStruct((sec_dev, rows, LANES), F32)),
        in_specs=[
            SCALARS,
            SCALARS,
            section_spec(after.shape),
            section_spec(after_low.shape),
            section_spec(after_high.shape),
            whole_spec(along.shape),
            whole_spec(down.shape),
            whole_spec(form_rows.shape),
            whole_spec(form_cols.shape),
            coef_spec,
            coef_spec,
            section_spec(fwd_offset.shape),
            section_spec(bwd_offset.shape),
            section_spec(valid.shape),
        ],
        out_specs=(section_spec(flow_shape.shape), section_spec((sec_dev, rows, LANES))),
        scratch_shapes=[
            pltpu.VMEM((height + 2 * OFFMAX + 8, width + 2 * LANES), F32),
            pltpu.VMEM((2, height, 2 * LANES), BF),
            pltpu.VMEM((2, rows, 2 * PATCH, 2 * PATCH), BF),
            pltpu.VMEM((2, PATCH, 2 * PATCH), F32),
            pltpu.VMEM((2, PATCH, 2 * PATCH), F32),
            pltpu.VMEM((2, 2, PATCH, 2 * PATCH), F32),
            pltpu.VMEM((2, 2, 2 * PATCH, 2 * PATCH), BF),
            pltpu.VMEM((6, pairs, rows, LANES), F32),
        ],
        compiler_params=PARAMS,
        cost_estimate=cost(2 * 10**10),
        name="pair_flows",
    )(notlast, fwd_offset, after, after_low, after_high, along, down, form_rows, form_cols,
      own_patch, own_window, fwd_offset, bwd_offset, valid)


def body(image, fwd_offset, bwd_offset, valid):
    sec_dev, height, width = image.shape
    rows, count = valid.shape[1:]
    pairs = count // 2
    sec_size, tile_size = lax.axis_size("sec"), lax.axis_size("tile")
    sections = sec_dev * sec_size
    earlier = [(i, i - 1) for i in range(1, sec_size)]
    arriving = lax.ppermute(image[:1], "sec", earlier)
    up = [(i, i + 1) for i in range(tile_size - 1)]
    back = [(i + 1, i) for i in range(tile_size - 1)]
    low = lax.ppermute(image[:, -OFFMAX:], "tile", up)
    high = lax.ppermute(image[:, :OFFMAX], "tile", back)
    edges = lax.ppermute(jnp.concatenate([low[:1], high[:1]], 1), "sec", earlier)
    after = jnp.concatenate([image[1:], arriving], 0)
    after_low = jnp.concatenate([low[1:], edges[:, :OFFMAX]], 0)
    after_high = jnp.concatenate([high[1:], edges[:, OFFMAX:]], 0)

    own_patch = patch_spectra(image, rows, pairs)
    own_window = window_spectra(bwd_offset, image, low, high, rows, pairs)
    place = lax.axis_index("sec") * sec_dev
    notlast = (place + jnp.arange(sec_dev, dtype=jnp.int32) < sections - 1).astype(jnp.int32)
    pair_flow, tile = pair_flows(
        notlast, fwd_offset, after, after_low, after_high, own_patch, own_window, bwd_offset, valid
    )
    devices = sec_size * tile_size
    everywhere = lax.all_to_all(jnp.broadcast_to(tile[None], (devices,) + tile.shape), ("sec", "tile"), 0, 0)
    everywhere = (
        everywhere.reshape(sec_size, tile_size, sec_dev, rows, LANES)
        .transpose(0, 2, 1, 3, 4)
        .reshape(sections, tile_size * rows, LANES)
    )
    where = jnp.stack([place, lax.axis_index("tile") * rows]).astype(jnp.int32)
    mesh_shift = pl.pallas_call(
        mesh_kernel,
        out_shape=jax.ShapeDtypeStruct(pair_flow.shape, F32),
        in_specs=[SCALARS, pl.BlockSpec(memory_space=pltpu.VMEM)],
        out_specs=pl.BlockSpec(memory_space=pltpu.VMEM),
        scratch_shapes=[pltpu.VMEM((sections, tile_size * rows, LANES), F32)],
        compiler_params=pltpu.CompilerParams(vmem_limit_bytes=8 * 1024 * 1024),
        name="relax",
    )(where, everywhere)
    return pair_flow, mesh_shift


def solution(mesh):
    return jax.shard_map(
        body,
        mesh=mesh,
        in_specs=(
            P("sec", "tile", None),
            P("sec", None, "tile", None),
            P("sec", None, "tile", None),
            P("sec", "tile", None),
        ),
        out_specs=(P("sec", None, "tile", None), P("sec", None, "tile", None)),
        check_vma=False,
    )
```

```python
import functools

import jax
import jax.numpy as jnp
import ml_dtypes
import numpy as np
from jax import lax
from jax.experimental import pallas as pl
from jax.experimental.pallas import tpu as pltpu
from jax.sharding import PartitionSpec as P

PATCH = 128
HALF = PATCH // 2
OFFMAX = 16
ITERS = 3
LANES = 128
BF = jnp.bfloat16
F32 = jnp.float32


def split_table(table):
    high = table.astype(np.float32).astype(ml_dtypes.bfloat16)
    low = (table - high.astype(np.float64)).astype(np.float32).astype(ml_dtypes.bfloat16)
    return high, low


@functools.cache
def tables():
    place = np.arange(PATCH)
    quarter = np.sin(np.arange(PATCH // 4 + 1) * (2 * np.pi / PATCH))
    sine = np.concatenate([quarter, quarter[-2::-1], -quarter[1:], -quarter[-2:0:-1]])
    cosine = np.roll(sine, -PATCH // 4)
    basis = np.zeros((PATCH, PATCH))
    basis[0] = place % 2 == 0
    basis[HALF] = place % 2 == 1
    for u in range(1, HALF):
        basis[u] = cosine[(u * place) % PATCH]
        basis[HALF + u] = sine[(u * place) % PATCH]
    lag = ((place + HALF) % PATCH) - HALF
    full = (basis * lag) @ basis.T
    form = np.zeros((HALF, PATCH))
    form[1:] = 2 * full[HALF + 1 :]
    form[1:, HALF + 1 :] = 0
    form[0, :HALF] = basis[:HALF, HALF]
    basis_high, basis_low = split_table(basis)
    form_high, form_low = split_table(form)

    def side_by_side(part):
        out = np.zeros((2 * PATCH, 2 * PATCH), ml_dtypes.bfloat16)
        for t in range(2):
            for s in range(2):
                out[t * PATCH : (t + 1) * PATCH, s * PATCH + t * HALF : s * PATCH + (t + 1) * HALF] = (
                    part[s * HALF : (s + 1) * HALF].T
                )
        return out

    def columns(part):
        out = np.zeros((2 * PATCH, PATCH), ml_dtypes.bfloat16)
        for t in range(2):
            for s in range(2):
                out[s * PATCH + t * HALF : s * PATCH + (t + 1) * HALF, t * HALF : (t + 1) * HALF] = (
                    part[:, s * HALF : (s + 1) * HALF].T
                )
        return out

    along = np.concatenate([side_by_side(basis_high), side_by_side(basis_low)], 0)
    down = np.concatenate(
        [np.concatenate([basis_high, basis_high], 1), np.concatenate([basis_low, basis_low * 0], 1)], 0
    )
    form_rows = np.concatenate(
        [np.concatenate([form_high, form_high], 1), np.concatenate([form_low, form_low * 0], 1)], 0
    )
    form_cols = np.concatenate([columns(form_high), columns(form_low)], 1)
    return along, down, form_rows, form_cols


def dot(a, b):
    return jnp.dot(a, b, preferred_element_type=F32)


def split(x):
    high = x.astype(BF)
    return high, (x - high.astype(F32)).astype(BF)


def fill_padded(padded, image_ref, low_ref, high_ref):
    rows, cols = image_ref.shape
    padded[:, 0:LANES] = jnp.zeros((padded.shape[0], LANES), F32)
    padded[:, LANES + cols :] = jnp.zeros((padded.shape[0], LANES), F32)
    padded[2 * OFFMAX + rows :, :] = jnp.zeros((8, padded.shape[1]), F32)
    padded[0:OFFMAX, LANES : LANES + cols] = low_ref[...].astype(F32)
    padded[OFFMAX + rows : 2 * OFFMAX + rows, LANES : LANES + cols] = high_ref[...].astype(F32)

    def step(i, carry):
        r = pl.multiple_of(i * 64, 64)
        padded[pl.ds(r + OFFMAX, 64), LANES : LANES + cols] = image_ref[pl.ds(r, 64), :].astype(F32)
        return carry

    lax.fori_loop(0, rows // 64, step, 0)


def fill_window_row(window, padded, off_ref, s, c, i):
    lane = lax.broadcasted_iota(jnp.int32, (PATCH + 8, LANES), 1)
    deep = lax.broadcasted_iota(jnp.int32, (PATCH // 8, 8, LANES), 1)
    for t in range(2):
        j = 2 * c + t
        top = OFFMAX + off_ref[s, 0, i, j]
        ox = off_ref[s, 1, i, j]
        left = (ox < 0).astype(jnp.int32)
        base = pl.multiple_of((j + 1 - left) * LANES, LANES)
        shift = ox + LANES * left
        aligned = pl.multiple_of(i * PATCH + jnp.bitwise_and(top, -8), 8)
        block = padded[pl.ds(aligned, PATCH + 8), pl.ds(base, 2 * LANES)]
        turn = jnp.bitwise_and(LANES - shift, LANES - 1)
        first = pltpu.roll(block[:, :LANES], turn, 1)
        second = pltpu.roll(block[:, LANES:], turn, 1)
        cut = jnp.where(lane < LANES - shift, first, second)
        over = jnp.bitwise_and(top, 7)
        cut = pltpu.roll(cut.reshape(PATCH // 8 + 1, 8, LANES), jnp.bitwise_and(8 - over, 7), 1)
        cut = jnp.where(deep < 8 - over, cut[:-1], cut[1:]).reshape(PATCH, LANES)
        window[i * PATCH : (i + 1) * PATCH, t * LANES : (t + 1) * LANES] = cut.astype(BF)


def first_stage(block, along_ref, parts):
    high, low = split(dot(jnp.concatenate([block, block], 1), along_ref[...]))
    rows = parts.shape[0]
    parts[:, :PATCH] = high.reshape(rows, PATCH, 2 * PATCH)
    parts[:, PATCH:] = low.reshape(rows, PATCH, 2 * PATCH)


def second_stage(part, down_ref):
    both = dot(down_ref[...], part)
    return both[:PATCH] + both[PATCH:]


def store_coefficients(out_ref, coef):
    row = lax.broadcasted_iota(jnp.int32, (8, LANES), 0)
    lane = lax.broadcasted_iota(jnp.int32, (8, LANES), 1)
    corner = jnp.logical_and(row == 0, lane % HALF == 0)
    out_ref[...] = coef
    mean = 0.25 * (
        coef[0:8, :LANES] + coef[0:8, LANES:] + coef[HALF : HALF + 8, :LANES] + coef[HALF : HALF + 8, LANES:]
    )
    mean = jnp.where(corner, mean, 0.0)
    for r in (0, HALF):
        for q in (0, LANES):
            out_ref[r : r + 8, q : q + LANES] = coef[r : r + 8, q : q + LANES] - mean


def patch_kernel(image_ref, along_ref, down_ref, out_ref, parts):
    rows = image_ref.shape[0] // PATCH
    s, c = pl.program_id(0), pl.program_id(1)
    first_stage(image_ref[...], along_ref, parts)
    for i in range(rows):
        store_coefficients(out_ref.at[s, c, i], second_stage(parts[i], down_ref))


def window_kernel(off_ref, image_ref, low_ref, high_ref, along_ref, down_ref, out_ref, padded, window, parts):
    s, c = pl.program_id(0), pl.program_id(1)
    rows = image_ref.shape[0] // PATCH

    @pl.when(c == 0)
    def _():
        fill_padded(padded, image_ref, low_ref, high_ref)
        for i in range(rows):
            fill_window_row(window.at[0], padded, off_ref, s, 0, i)

    first_stage(window[c % 2], along_ref, parts)
    following = jnp.minimum(c + 1, pl.num_programs(1) - 1)
    for i in range(rows):
        store_coefficients(out_ref.at[s, c, i], second_stage(parts[i], down_ref))
        fill_window_row(window.at[(c + 1) % 2], padded, off_ref, s, following, i)


def cross(a_ref, b_ref, coef, pieces):
    lane = lax.broadcasted_iota(jnp.int32, (16, LANES), 1)
    row = lax.broadcasted_iota(jnp.int32, (16, LANES), 0)
    sign_j = jnp.where(lane % HALF == 0, -1.0, 1.0).astype(F32)
    first_row = jnp.where(row == 0, -1.0, 1.0).astype(F32)
    total = jnp.zeros((16, LANES), F32)
    for g in range(HALF // 16):
        top, bottom = slice(16 * g, 16 * g + 16), slice(HALF + 16 * g, HALF + 16 * g + 16)
        acc, acs, asc, ass = a_ref[top, :LANES], a_ref[top, LANES:], a_ref[bottom, :LANES], a_ref[bottom, LANES:]
        bcc, bcs, bsc, bss = b_ref[top, :LANES], b_ref[top, LANES:], b_ref[bottom, :LANES], b_ref[bottom, LANES:]
        acs_j, ass_j = acs * sign_j, ass * sign_j
        cc = acc * bcc + acs * bcs + asc * bsc + ass * bss
        cs = acc * bcs + asc * bss - (acs_j * bcc + ass_j * bsc)
        turned_sc = asc * bcc + ass * bcs
        turned_ss = asc * bcs - ass_j * bcc
        if g == 0:
            turned_sc, turned_ss = turned_sc * first_row, turned_ss * first_row
        sc = acc * bsc + acs * bss - turned_sc
        ss = acc * bss - acs_j * bsc - turned_ss
        total = total + (cc * cc + cs * cs + sc * sc + ss * ss)
        for where, lanes, value in (
            (top, slice(0, LANES), cc),
            (top, slice(LANES, 2 * LANES), cs),
            (bottom, slice(0, LANES), sc),
            (bottom, slice(LANES, 2 * LANES), ss),
        ):
            high, low = split(value)
            coef[where, lanes] = value
            pieces[where, lanes] = high
            pieces[slice(PATCH + where.start, PATCH + where.stop), lanes] = low
    return jnp.sum(total, axis=0, keepdims=True)


def moments(coef, pieces, rows_ref, cols_ref):
    down = dot(rows_ref[...], pieces[...])
    across = dot(pieces[...], cols_ref[...])
    down = down[:HALF] + down[HALF:]
    across = across[:PATCH, :LANES] + across[:PATCH, LANES:] + across[PATCH:, :LANES]
    row8 = lax.broadcasted_iota(jnp.int32, (8, 2 * LANES), 0)
    head = down[0:8]
    moment_r = jnp.where(row8 == 0, -float(HALF) * head, coef[HALF : HALF + 8, :]) * head
    for g in range(1, HALF // 8):
        moment_r = moment_r + down[8 * g : 8 * g + 8] * coef[HALF + 8 * g : HALF + 8 * g + 8, :]
    moment_r = moment_r[:, :LANES] + moment_r[:, LANES:]
    lane8 = lax.broadcasted_iota(jnp.int32, (8, LANES), 1) % HALF == 0
    moment_c = jnp.zeros((8, LANES), F32)
    for g in range(PATCH // 8):
        piece = across[8 * g : 8 * g + 8]
        other = jnp.where(lane8, -float(HALF) * piece, coef[8 * g : 8 * g + 8, LANES:])
        moment_c = moment_c + other * piece
    return jnp.sum(moment_r, axis=0, keepdims=True), jnp.sum(moment_c, axis=0, keepdims=True)


def pair_kernel(
    place_ref, off_ref, image_ref, low_ref, high_ref, along_ref, down_ref, rows_ref, cols_ref,
    own_patch, own_window, fwd_ref, bwd_ref, valid_ref, flow_out, tile_out,
    padded, window, parts, left, right, coef, pieces, sums,
):
    s, c = pl.program_id(0), pl.program_id(1)
    rows = image_ref.shape[0] // PATCH
    pairs = pl.num_programs(1)

    @pl.when(c == 0)
    def _():
        fill_padded(padded, image_ref, low_ref, high_ref)
        for i in range(rows):
            fill_window_row(window.at[0], padded, off_ref, s, 0, i)

    lanes = pl.ds(pl.multiple_of(c * 2 * LANES, 2 * LANES), 2 * LANES)
    first_stage(image_ref[:, lanes], along_ref, parts.at[0])
    first_stage(window[c % 2], along_ref, parts.at[1])
    following = jnp.minimum(c + 1, pairs - 1)

    def spectra(i):
        store_coefficients(left.at[i % 2], second_stage(parts[0, i], down_ref))
        store_coefficients(right.at[i % 2], second_stage(parts[1, i], down_ref))

    def products(i):
        k = i % 2
        sums[0, c, i : i + 1, :] = cross(own_patch.at[s, c, i], right.at[k], coef.at[0, k], pieces.at[0, k])
        sums[3, c, i : i + 1, :] = cross(left.at[k], own_window.at[s, c, i], coef.at[1, k], pieces.at[1, k])

    def centroid(i):
        for d in range(2):
            by_row, by_col = moments(coef.at[d, i % 2], pieces.at[d, i % 2], rows_ref, cols_ref)
            sums[3 * d + 1, c, i : i + 1, :] = by_row
            sums[3 * d + 2, c, i : i + 1, :] = by_col

    spectra(0)
    for i in range(rows):
        if i + 1 < rows:
            spectra(i + 1)
        products(i)
        fill_window_row(window.at[(c + 1) % 2], padded, off_ref, s, following, i)
        if i:
            centroid(i - 1)
    centroid(rows - 1)

    @pl.when(c == pairs - 1)
    def _():
        count = 2 * sums.shape[1]
        lane = lax.broadcasted_iota(jnp.int32, (rows, LANES), 1)
        gathered = []
        for k in range(6):
            value = jnp.zeros((rows, LANES), F32)
            for p in range(sums.shape[1]):
                held = sums[k, p]
                for t in range(2):
                    mine = (lane >= HALF) if t else (lane < HALF)
                    value = jnp.where(
                        lane == 2 * p + t, jnp.sum(jnp.where(mine, held, 0.0), axis=1, keepdims=True), value
                    )
            gathered.append(value[:, :count])
        scale = (2.0 / PATCH) ** 4 * HALF * HALF
        lag_scale = scale / HALF
        eps = PATCH * PATCH * 1e-6
        notlast = place_ref[s].astype(F32)
        weight = valid_ref[...].astype(F32) * notlast
        flows = []
        for comp in range(2):
            fwd = gathered[1 + comp] * lag_scale / (gathered[0] * scale + eps) + fwd_ref[comp].astype(F32)
            bwd = gathered[4 + comp] * lag_scale / (gathered[3] * scale + eps) + bwd_ref[comp].astype(F32)
            flow = 0.5 * (fwd - bwd) * notlast
            flow_out[comp] = flow
            flows.append(flow)
        fill = jnp.zeros((rows, LANES - 4 * count), F32)
        wide = jnp.concatenate(flows + [weight, weight, fill], axis=1)
        row = lax.broadcasted_iota(jnp.int32, (rows, LANES), 0)
        group = 2 * count
        packed = []
        for begin in (0, group):
            line = jnp.zeros((rows, LANES), F32)
            for i in range(rows):
                turned = pltpu.roll(wide, (group * i - begin) % LANES, 1)
                line = jnp.where(jnp.logical_and(row == i, lane // group == i), turned, line)
            packed.append(jnp.sum(line, axis=0, keepdims=True))
        packed = jnp.concatenate(packed, axis=0)
        for k in range(tile_out.shape[0]):
            tile_out[k, s] = packed


def mesh_kernel(tiles, place_ref, all_ref, shift_out):
    bands = all_ref.shape[0]
    sec_dev, _, rows, count = shift_out.shape
    group = 2 * count
    assert rows * group == LANES
    everything = all_ref[...]
    flow, weight = everything[:, 0], everything[:, 1]
    line = lax.broadcasted_iota(jnp.int32, (bands, LANES), 0)
    lane = lax.broadcasted_iota(jnp.int32, (bands, LANES), 1)
    band = line % tiles
    col, is_x, patch_row = lane % count, lane // count % 2, lane // group
    pulled = weight * flow

    def over_section(x):
        total = x
        for k in range(1, tiles):
            total = total + jnp.where(band >= k, pltpu.roll(x, k, 0), pltpu.roll(x, bands - tiles + k, 0))
        return total

    sum_y = jnp.sum(jnp.where(is_x == 0, pulled, 0.0), axis=1, keepdims=True)
    sum_x = jnp.sum(jnp.where(is_x == 1, pulled, 0.0), axis=1, keepdims=True)
    counts = jnp.sum(jnp.where(is_x == 0, weight, 0.0), axis=1, keepdims=True)
    sums = over_section(jnp.where(is_x == 0, sum_y, sum_x))
    mean = sums / jnp.maximum(over_section(jnp.broadcast_to(counts, sums.shape)), 1.0)
    shift = jnp.where(line >= tiles, pltpu.roll(mean, tiles, 0), 0.0)
    reach = tiles
    while reach < bands:
        shift = shift + jnp.where(line >= reach, pltpu.roll(shift, reach, 0), 0.0)
        reach *= 2
    at_top, at_bottom = patch_row == 0, patch_row == rows - 1
    one = lambda condition: condition.astype(F32)
    has_left, has_right = one(col > 0), one(col < count - 1)
    has_up = one(jnp.logical_or(band > 0, patch_row > 0))
    has_down = one(jnp.logical_or(band < tiles - 1, patch_row < rows - 1))
    degree = has_left + has_right + has_up + has_down
    not_first = one(line >= tiles)
    not_end = one(line < bands - tiles)
    weight_next, pulled_next = weight * not_end, pulled
    for _ in range(ITERS):
        lower, upper = pltpu.roll(shift, group, 1), pltpu.roll(shift, LANES - group, 1)
        above = jnp.where(at_top, pltpu.roll(lower, 1, 0), lower)
        below = jnp.where(at_bottom, pltpu.roll(upper, bands - 1, 0), upper)
        plane = (
            has_up * above
            + has_down * below
            + has_left * pltpu.roll(shift, 1, 1)
            + has_right * pltpu.roll(shift, LANES - 1, 1)
            - degree * shift
        )
        spring = weight_next * (pltpu.roll(shift, bands - tiles, 0) - shift) - pulled_next
        between = spring - not_first * pltpu.roll(spring, tiles, 0)
        shift = shift + 0.25 * (plane + between)
    mine_line = lax.broadcasted_iota(jnp.int32, (bands, LANES), 0)
    row = lax.broadcasted_iota(jnp.int32, (rows, LANES), 0)
    for k in range(sec_dev):
        mine = jnp.sum(jnp.where(mine_line == place_ref[0] + k * tiles, shift, 0.0), axis=0, keepdims=True)
        spread = jnp.zeros((rows, LANES), F32)
        wide = jnp.broadcast_to(mine, (rows, LANES))
        for i in range(rows):
            spread = jnp.where(row == i, pltpu.roll(wide, (LANES - group * i) % LANES, 1), spread)
        shift_out[k, 0] = spread[:, :count]
        shift_out[k, 1] = spread[:, count:group]


def section_spec(shape):
    return pl.BlockSpec((None,) + shape[1:], lambda s, c: (s,) + (0,) * (len(shape) - 1))


def whole_spec(shape):
    return pl.BlockSpec(shape, lambda s, c: (0,) * len(shape))


SCALARS = pl.BlockSpec(memory_space=pltpu.SMEM)


PARAMS = pltpu.CompilerParams(vmem_limit_bytes=24 * 1024 * 1024)


def in_hbm(array):
    return pltpu.with_memory_space_constraint(array, pltpu.HBM)


def cost(flops):
    return pl.CostEstimate(flops=flops, bytes_accessed=10**7, transcendentals=0)


def coef_layout(sec_dev, rows, pairs):
    return pltpu.VMEM((sec_dev, pairs, rows, PATCH, 2 * PATCH), F32), pl.BlockSpec(memory_space=pltpu.VMEM)


def patch_spectra(image, rows, pairs):
    sec_dev, height, width = image.shape
    along, down, _, _ = (jnp.asarray(t) for t in tables())
    shape, spec = coef_layout(sec_dev, rows, pairs)
    return pl.pallas_call(
        patch_kernel,
        grid=(sec_dev, pairs),
        out_shape=shape,
        in_specs=[
            pl.BlockSpec((None, height, 2 * LANES), lambda s, c: (s, 0, c)),
            whole_spec(along.shape),
            whole_spec(down.shape),
        ],
        out_specs=spec,
        scratch_shapes=[pltpu.VMEM((rows, 2 * PATCH, 2 * PATCH), BF)],
        compiler_params=PARAMS,
        cost_estimate=cost(5 * 10**9),
        name="patch_spectra",
    )(*(in_hbm(x) for x in (image, along, down)))


def window_spectra(offset, image, low, high, rows, pairs):
    sec_dev, height, width = image.shape
    along, down, _, _ = (jnp.asarray(t) for t in tables())
    shape, spec = coef_layout(sec_dev, rows, pairs)
    return pl.pallas_call(
        window_kernel,
        grid=(sec_dev, pairs),
        out_shape=shape,
        in_specs=[
            SCALARS,
            section_spec(image.shape),
            section_spec(low.shape),
            section_spec(high.shape),
            whole_spec(along.shape),
            whole_spec(down.shape),
        ],
        out_specs=spec,
        scratch_shapes=[
            pltpu.VMEM((height + 2 * OFFMAX + 8, width + 2 * LANES), F32),
            pltpu.VMEM((2, height, 2 * LANES), BF),
            pltpu.VMEM((rows, 2 * PATCH, 2 * PATCH), BF),
        ],
        compiler_params=PARAMS,
        cost_estimate=cost(5 * 10**9),
        name="window_spectra",
    )(offset, image, low, high, along, down)


def pair_flows(devices, notlast, fwd_offset, after, after_low, after_high, own_patch, own_window, bwd_offset, valid):
    sec_dev, height, width = after.shape
    rows, count = valid.shape[1:]
    pairs = count // 2
    along, down, form_rows, form_cols = (jnp.asarray(t) for t in tables())
    _, coef_spec = coef_layout(sec_dev, rows, pairs)
    flow_shape = jax.ShapeDtypeStruct((sec_dev, 2, rows, count), F32)
    return pl.pallas_call(
        pair_kernel,
        grid=(sec_dev, pairs),
        out_shape=(flow_shape, jax.ShapeDtypeStruct((devices, sec_dev, 2, LANES), F32)),
        in_specs=[
            SCALARS,
            SCALARS,
            section_spec(after.shape),
            section_spec(after_low.shape),
            section_spec(after_high.shape),
            whole_spec(along.shape),
            whole_spec(down.shape),
            whole_spec(form_rows.shape),
            whole_spec(form_cols.shape),
            coef_spec,
            coef_spec,
            section_spec(fwd_offset.shape),
            section_spec(bwd_offset.shape),
            section_spec(valid.shape),
        ],
        out_specs=(section_spec(flow_shape.shape), pl.BlockSpec(memory_space=pltpu.VMEM)),
        scratch_shapes=[
            pltpu.VMEM((height + 2 * OFFMAX + 8, width + 2 * LANES), F32),
            pltpu.VMEM((2, height, 2 * LANES), BF),
            pltpu.VMEM((2, rows, 2 * PATCH, 2 * PATCH), BF),
            pltpu.VMEM((2, PATCH, 2 * PATCH), F32),
            pltpu.VMEM((2, PATCH, 2 * PATCH), F32),
            pltpu.VMEM((2, 2, PATCH, 2 * PATCH), F32),
            pltpu.VMEM((2, 2, 2 * PATCH, 2 * PATCH), BF),
            pltpu.VMEM((6, pairs, rows, LANES), F32),
        ],
        compiler_params=PARAMS,
        cost_estimate=cost(2 * 10**10),
        name="pair_flows",
    )(notlast, fwd_offset, after, after_low, after_high, along, down, form_rows, form_cols,
      own_patch, own_window, fwd_offset, bwd_offset, valid)


def body(image, fwd_offset, bwd_offset, valid):
    sec_dev, height, width = image.shape
    rows, count = valid.shape[1:]
    pairs = count // 2
    sec_size, tile_size = lax.axis_size("sec"), lax.axis_size("tile")
    sections = sec_dev * sec_size
    earlier = [(i, i - 1) for i in range(1, sec_size)]
    arriving = lax.ppermute(image[:1], "sec", earlier)
    up = [(i, i + 1) for i in range(tile_size - 1)]
    back = [(i + 1, i) for i in range(tile_size - 1)]
    low = lax.ppermute(image[:, -OFFMAX:], "tile", up)
    high = lax.ppermute(image[:, :OFFMAX], "tile", back)
    edges = lax.ppermute(jnp.concatenate([low[:1], high[:1]], 1), "sec", earlier)
    after = jnp.concatenate([image[1:], arriving], 0)
    after_low = jnp.concatenate([low[1:], edges[:, :OFFMAX]], 0)
    after_high = jnp.concatenate([high[1:], edges[:, OFFMAX:]], 0)

    own_patch = patch_spectra(image, rows, pairs)
    own_window = window_spectra(bwd_offset, image, low, high, rows, pairs)
    place = lax.axis_index("sec") * sec_dev
    notlast = (place + jnp.arange(sec_dev, dtype=jnp.int32) < sections - 1).astype(jnp.int32)
    pair_flow, tiles = pair_flows(
        sec_size * tile_size, notlast, fwd_offset, after, after_low, after_high, own_patch, own_window, bwd_offset, valid
    )
    everywhere = lax.all_to_all(tiles, ("sec", "tile"), 0, 0)
    everywhere = (
        everywhere.reshape(sec_size, tile_size, sec_dev, 2, LANES)
        .transpose(0, 2, 1, 3, 4)
        .reshape(sections * tile_size, 2, LANES)
    )
    where = (place * tile_size + lax.axis_index("tile")).astype(jnp.int32).reshape(1)
    mesh_shift = pl.pallas_call(
        functools.partial(mesh_kernel, tile_size),
        out_shape=jax.ShapeDtypeStruct(pair_flow.shape, F32),
        in_specs=[SCALARS, pl.BlockSpec(memory_space=pltpu.VMEM)],
        out_specs=pl.BlockSpec(memory_space=pltpu.VMEM),
        compiler_params=pltpu.CompilerParams(vmem_limit_bytes=8 * 1024 * 1024),
        name="relax",
    )(where, everywhere)
    return pair_flow, mesh_shift


def solution(mesh):
    return jax.shard_map(
        body,
        mesh=mesh,
        in_specs=(
            P("sec", "tile", None),
            P("sec", None, "tile", None),
            P("sec", None, "tile", None),
            P("sec", "tile", None),
        ),
        out_specs=(P("sec", None, "tile", None), P("sec", None, "tile", None)),
        check_vma=False,
    )
```

```python
import functools

import jax
import jax.numpy as jnp
import ml_dtypes
import numpy as np
from jax import lax
from jax.experimental import pallas as pl
from jax.experimental.pallas import tpu as pltpu
from jax.sharding import PartitionSpec as P

PATCH = 128
HALF = PATCH // 2
OFFMAX = 16
ITERS = 3
LANES = 128
BF = jnp.bfloat16
F32 = jnp.float32


def split_table(table):
    high = table.astype(np.float32).astype(ml_dtypes.bfloat16)
    low = (table - high.astype(np.float64)).astype(np.float32).astype(ml_dtypes.bfloat16)
    return high, low


@functools.cache
def tables():
    place = np.arange(PATCH)
    quarter = np.sin(np.arange(PATCH // 4 + 1) * (2 * np.pi / PATCH))
    sine = np.concatenate([quarter, quarter[-2::-1], -quarter[1:], -quarter[-2:0:-1]])
    cosine = np.roll(sine, -PATCH // 4)
    basis = np.zeros((PATCH, PATCH))
    basis[0] = place % 2 == 0
    basis[HALF] = place % 2 == 1
    for u in range(1, HALF):
        basis[u] = cosine[(u * place) % PATCH]
        basis[HALF + u] = sine[(u * place) % PATCH]
    lag = ((place + HALF) % PATCH) - HALF
    full = (basis * lag) @ basis.T
    form = np.zeros((HALF, PATCH))
    form[1:] = 2 * full[HALF + 1 :]
    form[1:, HALF + 1 :] = 0
    form[0, :HALF] = basis[:HALF, HALF]
    basis_high, basis_low = split_table(basis)
    form_high, form_low = split_table(form)

    def side_by_side(part):
        out = np.zeros((2 * PATCH, 2 * PATCH), ml_dtypes.bfloat16)
        for t in range(2):
            for s in range(2):
                out[t * PATCH : (t + 1) * PATCH, s * PATCH + t * HALF : s * PATCH + (t + 1) * HALF] = (
                    part[s * HALF : (s + 1) * HALF].T
                )
        return out

    def columns(part):
        out = np.zeros((2 * PATCH, PATCH), ml_dtypes.bfloat16)
        for t in range(2):
            for s in range(2):
                out[s * PATCH + t * HALF : s * PATCH + (t + 1) * HALF, t * HALF : (t + 1) * HALF] = (
                    part[:, s * HALF : (s + 1) * HALF].T
                )
        return out

    along = np.concatenate([side_by_side(basis_high), side_by_side(basis_low)], 0)
    down = np.concatenate(
        [np.concatenate([basis_high, basis_high], 1), np.concatenate([basis_low, basis_low * 0], 1)], 0
    )
    form_rows = np.concatenate(
        [np.concatenate([form_high, form_high], 1), np.concatenate([form_low, form_low * 0], 1)], 0
    )
    form_cols = np.concatenate([columns(form_high), columns(form_low)], 1)
    return along, down, form_rows, form_cols


def dot(a, b):
    return jnp.dot(a, b, preferred_element_type=F32)


def split(x):
    high = x.astype(BF)
    return high, (x - high.astype(F32)).astype(BF)


def fill_padded(padded, image_ref, low_ref, high_ref):
    rows, cols = image_ref.shape
    padded[:, 0:LANES] = jnp.zeros((padded.shape[0], LANES), F32)
    padded[:, LANES + cols :] = jnp.zeros((padded.shape[0], LANES), F32)
    padded[2 * OFFMAX + rows :, :] = jnp.zeros((8, padded.shape[1]), F32)
    padded[0:OFFMAX, LANES : LANES + cols] = low_ref[...].astype(F32)
    padded[OFFMAX + rows : 2 * OFFMAX + rows, LANES : LANES + cols] = high_ref[...].astype(F32)

    def step(i, carry):
        r = pl.multiple_of(i * 64, 64)
        padded[pl.ds(r + OFFMAX, 64), LANES : LANES + cols] = image_ref[pl.ds(r, 64), :].astype(F32)
        return carry

    lax.fori_loop(0, rows // 64, step, 0)


def fill_window_row(window, padded, off_ref, s, c, i):
    lane = lax.broadcasted_iota(jnp.int32, (PATCH + 8, LANES), 1)
    deep = lax.broadcasted_iota(jnp.int32, (PATCH // 8, 8, LANES), 1)
    for t in range(2):
        j = 2 * c + t
        top = OFFMAX + off_ref[s, 0, i, j]
        ox = off_ref[s, 1, i, j]
        left = (ox < 0).astype(jnp.int32)
        base = pl.multiple_of((j + 1 - left) * LANES, LANES)
        shift = ox + LANES * left
        aligned = pl.multiple_of(i * PATCH + jnp.bitwise_and(top, -8), 8)
        block = padded[pl.ds(aligned, PATCH + 8), pl.ds(base, 2 * LANES)]
        turn = jnp.bitwise_and(LANES - shift, LANES - 1)
        first = pltpu.roll(block[:, :LANES], turn, 1)
        second = pltpu.roll(block[:, LANES:], turn, 1)
        cut = jnp.where(lane < LANES - shift, first, second)
        over = jnp.bitwise_and(top, 7)
        cut = pltpu.roll(cut.reshape(PATCH // 8 + 1, 8, LANES), jnp.bitwise_and(8 - over, 7), 1)
        cut = jnp.where(deep < 8 - over, cut[:-1], cut[1:]).reshape(PATCH, LANES)
        window[i * PATCH : (i + 1) * PATCH, t * LANES : (t + 1) * LANES] = cut.astype(BF)


def first_stage(block, along_ref, parts):
    high, low = split(dot(jnp.concatenate([block, block], 1), along_ref[...]))
    rows = parts.shape[0]
    parts[:, :PATCH] = high.reshape(rows, PATCH, 2 * PATCH)
    parts[:, PATCH:] = low.reshape(rows, PATCH, 2 * PATCH)


def second_stage(part, down_ref):
    both = dot(down_ref[...], part)
    return both[:PATCH] + both[PATCH:]


def store_coefficients(out_ref, coef):
    row = lax.broadcasted_iota(jnp.int32, (8, LANES), 0)
    lane = lax.broadcasted_iota(jnp.int32, (8, LANES), 1)
    corner = jnp.logical_and(row == 0, lane % HALF == 0)
    out_ref[...] = coef
    mean = 0.25 * (
        coef[0:8, :LANES] + coef[0:8, LANES:] + coef[HALF : HALF + 8, :LANES] + coef[HALF : HALF + 8, LANES:]
    )
    mean = jnp.where(corner, mean, 0.0)
    for r in (0, HALF):
        for q in (0, LANES):
            out_ref[r : r + 8, q : q + LANES] = coef[r : r + 8, q : q + LANES] - mean


def patch_kernel(image_ref, along_ref, down_ref, out_ref, parts):
    rows = image_ref.shape[0] // PATCH
    s, c = pl.program_id(0), pl.program_id(1)
    first_stage(image_ref[...], along_ref, parts)
    for i in range(rows):
        store_coefficients(out_ref.at[s, c, i], second_stage(parts[i], down_ref))


def window_kernel(off_ref, image_ref, low_ref, high_ref, along_ref, down_ref, out_ref, padded, window, parts):
    s, c = pl.program_id(0), pl.program_id(1)
    rows = image_ref.shape[0] // PATCH

    @pl.when(c == 0)
    def _():
        fill_padded(padded, image_ref, low_ref, high_ref)
        for i in range(rows):
            fill_window_row(window.at[0], padded, off_ref, s, 0, i)

    first_stage(window[c % 2], along_ref, parts)
    following = jnp.minimum(c + 1, pl.num_programs(1) - 1)
    for i in range(rows):
        store_coefficients(out_ref.at[s, c, i], second_stage(parts[i], down_ref))
        fill_window_row(window.at[(c + 1) % 2], padded, off_ref, s, following, i)


def cross(a_ref, b_ref, coef, pieces):
    lane = lax.broadcasted_iota(jnp.int32, (16, LANES), 1)
    row = lax.broadcasted_iota(jnp.int32, (16, LANES), 0)
    sign_j = jnp.where(lane % HALF == 0, -1.0, 1.0).astype(F32)
    first_row = jnp.where(row == 0, -1.0, 1.0).astype(F32)
    total = jnp.zeros((16, LANES), F32)
    for g in range(HALF // 16):
        top, bottom = slice(16 * g, 16 * g + 16), slice(HALF + 16 * g, HALF + 16 * g + 16)
        acc, acs, asc, ass = a_ref[top, :LANES], a_ref[top, LANES:], a_ref[bottom, :LANES], a_ref[bottom, LANES:]
        bcc, bcs, bsc, bss = b_ref[top, :LANES], b_ref[top, LANES:], b_ref[bottom, :LANES], b_ref[bottom, LANES:]
        acs_j, ass_j = acs * sign_j, ass * sign_j
        cc = acc * bcc + acs * bcs + asc * bsc + ass * bss
        cs = acc * bcs + asc * bss - (acs_j * bcc + ass_j * bsc)
        turned_sc = asc * bcc + ass * bcs
        turned_ss = asc * bcs - ass_j * bcc
        if g == 0:
            turned_sc, turned_ss = turned_sc * first_row, turned_ss * first_row
        sc = acc * bsc + acs * bss - turned_sc
        ss = acc * bss - acs_j * bsc - turned_ss
        total = total + (cc * cc + cs * cs + sc * sc + ss * ss)
        for where, lanes, value in (
            (top, slice(0, LANES), cc),
            (top, slice(LANES, 2 * LANES), cs),
            (bottom, slice(0, LANES), sc),
            (bottom, slice(LANES, 2 * LANES), ss),
        ):
            high, low = split(value)
            coef[where, lanes] = value
            pieces[where, lanes] = high
            pieces[slice(PATCH + where.start, PATCH + where.stop), lanes] = low
    return jnp.sum(total, axis=0, keepdims=True)


def moments(coef, pieces, rows_ref, cols_ref):
    down = dot(rows_ref[...], pieces[...])
    across = dot(pieces[...], cols_ref[...])
    down = down[:HALF] + down[HALF:]
    across = across[:PATCH, :LANES] + across[:PATCH, LANES:] + across[PATCH:, :LANES]
    row8 = lax.broadcasted_iota(jnp.int32, (8, 2 * LANES), 0)
    head = down[0:8]
    moment_r = jnp.where(row8 == 0, -float(HALF) * head, coef[HALF : HALF + 8, :]) * head
    for g in range(1, HALF // 8):
        moment_r = moment_r + down[8 * g : 8 * g + 8] * coef[HALF + 8 * g : HALF + 8 * g + 8, :]
    moment_r = moment_r[:, :LANES] + moment_r[:, LANES:]
    lane8 = lax.broadcasted_iota(jnp.int32, (8, LANES), 1) % HALF == 0
    moment_c = jnp.zeros((8, LANES), F32)
    for g in range(PATCH // 8):
        piece = across[8 * g : 8 * g + 8]
        other = jnp.where(lane8, -float(HALF) * piece, coef[8 * g : 8 * g + 8, LANES:])
        moment_c = moment_c + other * piece
    return jnp.sum(moment_r, axis=0, keepdims=True), jnp.sum(moment_c, axis=0, keepdims=True)


def pair_kernel(
    place_ref, off_ref, image_ref, low_ref, high_ref, along_ref, down_ref, rows_ref, cols_ref,
    own_patch, own_window, fwd_ref, bwd_ref, valid_ref, flow_out, tile_out,
    padded, window, parts, left, right, coef, pieces, sums,
):
    s = pl.program_id(0)
    rows = image_ref.shape[0] // PATCH
    pairs = own_patch.shape[1]
    steps = pairs * rows

    def first_image(c):
        first_stage(image_ref[:, 2 * c * LANES : 2 * (c + 1) * LANES], along_ref, parts.at[c % 2, 0])

    def first_window(c):
        first_stage(window[c % 2], along_ref, parts.at[c % 2, 1])

    def cut(c, i):
        fill_window_row(window.at[c % 2], padded, off_ref, s, c, i)

    def spectra(n):
        c, i = divmod(n, rows)
        store_coefficients(left.at[n % 2], second_stage(parts[c % 2, 0, i], down_ref))
        store_coefficients(right.at[n % 2], second_stage(parts[c % 2, 1, i], down_ref))

    def products(n):
        c, i = divmod(n, rows)
        k = n % 2
        sums[0, c, i : i + 1, :] = cross(own_patch.at[s, c, i], right.at[k], coef.at[0, k], pieces.at[0, k])
        sums[3, c, i : i + 1, :] = cross(left.at[k], own_window.at[s, c, i], coef.at[1, k], pieces.at[1, k])

    def centroid(n):
        c, i = divmod(n, rows)
        for d in range(2):
            by_row, by_col = moments(coef.at[d, n % 2], pieces.at[d, n % 2], rows_ref, cols_ref)
            sums[3 * d + 1, c, i : i + 1, :] = by_row
            sums[3 * d + 2, c, i : i + 1, :] = by_col

    fill_padded(padded, image_ref, low_ref, high_ref)
    first_image(0)
    for i in range(rows):
        cut(0, i)
    first_window(0)
    spectra(0)
    early = max(rows - 2, 1)
    ready = [i * rows // early for i in range(early + 1)]
    for n in range(steps):
        c, i = divmod(n, rows)
        if c + 1 < pairs and i < early:
            for r in range(ready[i], ready[i + 1]):
                cut(c + 1, r)
            if i == 1:
                first_image(c + 1)
            if i == early - 1:
                first_window(c + 1)
        if n + 1 < steps:
            spectra(n + 1)
        products(n)
        if n:
            centroid(n - 1)
    centroid(steps - 1)

    count = 2 * sums.shape[1]
    lane = lax.broadcasted_iota(jnp.int32, (rows, LANES), 1)
    gathered = []
    for k in range(6):
        value = jnp.zeros((rows, LANES), F32)
        for p in range(sums.shape[1]):
            held = sums[k, p]
            for t in range(2):
                mine = (lane >= HALF) if t else (lane < HALF)
                value = jnp.where(
                    lane == 2 * p + t, jnp.sum(jnp.where(mine, held, 0.0), axis=1, keepdims=True), value
                )
        gathered.append(value[:, :count])
    scale = (2.0 / PATCH) ** 4 * HALF * HALF
    lag_scale = scale / HALF
    eps = PATCH * PATCH * 1e-6
    notlast = place_ref[s].astype(F32)
    weight = valid_ref[...].astype(F32) * notlast
    flows = []
    for comp in range(2):
        fwd = gathered[1 + comp] * lag_scale / (gathered[0] * scale + eps) + fwd_ref[comp].astype(F32)
        bwd = gathered[4 + comp] * lag_scale / (gathered[3] * scale + eps) + bwd_ref[comp].astype(F32)
        flow = 0.5 * (fwd - bwd) * notlast
        flow_out[comp] = flow
        flows.append(flow)
    fill = jnp.zeros((rows, LANES - 4 * count), F32)
    wide = jnp.concatenate(flows + [weight, weight, fill], axis=1)
    row = lax.broadcasted_iota(jnp.int32, (rows, LANES), 0)
    group = 2 * count
    packed = []
    for begin in (0, group):
        line = jnp.zeros((rows, LANES), F32)
        for i in range(rows):
            turned = pltpu.roll(wide, (group * i - begin) % LANES, 1)
            line = jnp.where(jnp.logical_and(row == i, lane // group == i), turned, line)
        packed.append(jnp.sum(line, axis=0, keepdims=True))
    packed = jnp.concatenate(packed, axis=0)
    for k in range(tile_out.shape[0]):
        tile_out[k, s] = packed


def mesh_kernel(tiles, place_ref, all_ref, shift_out):
    bands = all_ref.shape[0]
    sec_dev, _, rows, count = shift_out.shape
    group = 2 * count
    assert rows * group == LANES
    everything = all_ref[...]
    flow, weight = everything[:, 0], everything[:, 1]
    line = lax.broadcasted_iota(jnp.int32, (bands, LANES), 0)
    lane = lax.broadcasted_iota(jnp.int32, (bands, LANES), 1)
    band = line % tiles
    col, is_x, patch_row = lane % count, lane // count % 2, lane // group
    pulled = weight * flow

    def over_section(x):
        total = x
        for k in range(1, tiles):
            total = total + jnp.where(band >= k, pltpu.roll(x, k, 0), pltpu.roll(x, bands - tiles + k, 0))
        return total

    sum_y = jnp.sum(jnp.where(is_x == 0, pulled, 0.0), axis=1, keepdims=True)
    sum_x = jnp.sum(jnp.where(is_x == 1, pulled, 0.0), axis=1, keepdims=True)
    counts = jnp.sum(jnp.where(is_x == 0, weight, 0.0), axis=1, keepdims=True)
    sums = over_section(jnp.where(is_x == 0, sum_y, sum_x))
    mean = sums / jnp.maximum(over_section(jnp.broadcast_to(counts, sums.shape)), 1.0)
    shift = jnp.where(line >= tiles, pltpu.roll(mean, tiles, 0), 0.0)
    reach = tiles
    while reach < bands:
        shift = shift + jnp.where(line >= reach, pltpu.roll(shift, reach, 0), 0.0)
        reach *= 2
    at_top, at_bottom = patch_row == 0, patch_row == rows - 1
    one = lambda condition: condition.astype(F32)
    has_left, has_right = one(col > 0), one(col < count - 1)
    has_up = one(jnp.logical_or(band > 0, patch_row > 0))
    has_down = one(jnp.logical_or(band < tiles - 1, patch_row < rows - 1))
    degree = has_left + has_right + has_up + has_down
    not_first = one(line >= tiles)
    not_end = one(line < bands - tiles)
    weight_next, pulled_next = weight * not_end, pulled
    for _ in range(ITERS):
        lower, upper = pltpu.roll(shift, group, 1), pltpu.roll(shift, LANES - group, 1)
        above = jnp.where(at_top, pltpu.roll(lower, 1, 0), lower)
        below = jnp.where(at_bottom, pltpu.roll(upper, bands - 1, 0), upper)
        plane = (
            has_up * above
            + has_down * below
            + has_left * pltpu.roll(shift, 1, 1)
            + has_right * pltpu.roll(shift, LANES - 1, 1)
            - degree * shift
        )
        spring = weight_next * (pltpu.roll(shift, bands - tiles, 0) - shift) - pulled_next
        between = spring - not_first * pltpu.roll(spring, tiles, 0)
        shift = shift + 0.25 * (plane + between)
    mine_line = lax.broadcasted_iota(jnp.int32, (bands, LANES), 0)
    row = lax.broadcasted_iota(jnp.int32, (rows, LANES), 0)
    for k in range(sec_dev):
        mine = jnp.sum(jnp.where(mine_line == place_ref[0] + k * tiles, shift, 0.0), axis=0, keepdims=True)
        spread = jnp.zeros((rows, LANES), F32)
        wide = jnp.broadcast_to(mine, (rows, LANES))
        for i in range(rows):
            spread = jnp.where(row == i, pltpu.roll(wide, (LANES - group * i) % LANES, 1), spread)
        shift_out[k, 0] = spread[:, :count]
        shift_out[k, 1] = spread[:, count:group]


def section_spec(shape):
    return pl.BlockSpec((None,) + shape[1:], lambda s, *_: (s,) + (0,) * (len(shape) - 1))


def whole_spec(shape):
    return pl.BlockSpec(shape, lambda *_: (0,) * len(shape))


SCALARS = pl.BlockSpec(memory_space=pltpu.SMEM)


PARAMS = pltpu.CompilerParams(vmem_limit_bytes=24 * 1024 * 1024)


def in_hbm(array):
    return pltpu.with_memory_space_constraint(array, pltpu.HBM)


def cost(flops):
    return pl.CostEstimate(flops=flops, bytes_accessed=10**7, transcendentals=0)


def coef_layout(sec_dev, rows, pairs):
    return pltpu.VMEM((sec_dev, pairs, rows, PATCH, 2 * PATCH), F32), pl.BlockSpec(memory_space=pltpu.VMEM)


def patch_spectra(image, rows, pairs):
    sec_dev, height, width = image.shape
    along, down, _, _ = (jnp.asarray(t) for t in tables())
    shape, spec = coef_layout(sec_dev, rows, pairs)
    return pl.pallas_call(
        patch_kernel,
        grid=(sec_dev, pairs),
        out_shape=shape,
        in_specs=[
            pl.BlockSpec((None, height, 2 * LANES), lambda s, c: (s, 0, c)),
            whole_spec(along.shape),
            whole_spec(down.shape),
        ],
        out_specs=spec,
        scratch_shapes=[pltpu.VMEM((rows, 2 * PATCH, 2 * PATCH), BF)],
        compiler_params=PARAMS,
        cost_estimate=cost(5 * 10**9),
        name="patch_spectra",
    )(*(in_hbm(x) for x in (image, along, down)))


def window_spectra(offset, image, low, high, rows, pairs):
    sec_dev, height, width = image.shape
    along, down, _, _ = (jnp.asarray(t) for t in tables())
    shape, spec = coef_layout(sec_dev, rows, pairs)
    return pl.pallas_call(
        window_kernel,
        grid=(sec_dev, pairs),
        out_shape=shape,
        in_specs=[
            SCALARS,
            section_spec(image.shape),
            section_spec(low.shape),
            section_spec(high.shape),
            whole_spec(along.shape),
            whole_spec(down.shape),
        ],
        out_specs=spec,
        scratch_shapes=[
            pltpu.VMEM((height + 2 * OFFMAX + 8, width + 2 * LANES), F32),
            pltpu.VMEM((2, height, 2 * LANES), BF),
            pltpu.VMEM((rows, 2 * PATCH, 2 * PATCH), BF),
        ],
        compiler_params=PARAMS,
        cost_estimate=cost(5 * 10**9),
        name="window_spectra",
    )(offset, image, low, high, along, down)


def pair_flows(devices, notlast, fwd_offset, after, after_low, after_high, own_patch, own_window, bwd_offset, valid):
    sec_dev, height, width = after.shape
    rows, count = valid.shape[1:]
    pairs = count // 2
    along, down, form_rows, form_cols = (jnp.asarray(t) for t in tables())
    _, coef_spec = coef_layout(sec_dev, rows, pairs)
    flow_shape = jax.ShapeDtypeStruct((sec_dev, 2, rows, count), F32)
    return pl.pallas_call(
        pair_kernel,
        grid=(sec_dev,),
        out_shape=(flow_shape, jax.ShapeDtypeStruct((devices, sec_dev, 2, LANES), F32)),
        in_specs=[
            SCALARS,
            SCALARS,
            section_spec(after.shape),
            section_spec(after_low.shape),
            section_spec(after_high.shape),
            whole_spec(along.shape),
            whole_spec(down.shape),
            whole_spec(form_rows.shape),
            whole_spec(form_cols.shape),
            coef_spec,
            coef_spec,
            section_spec(fwd_offset.shape),
            section_spec(bwd_offset.shape),
            section_spec(valid.shape),
        ],
        out_specs=(section_spec(flow_shape.shape), pl.BlockSpec(memory_space=pltpu.VMEM)),
        scratch_shapes=[
            pltpu.VMEM((height + 2 * OFFMAX + 8, width + 2 * LANES), F32),
            pltpu.VMEM((2, height, 2 * LANES), BF),
            pltpu.VMEM((2, 2, rows, 2 * PATCH, 2 * PATCH), BF),
            pltpu.VMEM((2, PATCH, 2 * PATCH), F32),
            pltpu.VMEM((2, PATCH, 2 * PATCH), F32),
            pltpu.VMEM((2, 2, PATCH, 2 * PATCH), F32),
            pltpu.VMEM((2, 2, 2 * PATCH, 2 * PATCH), BF),
            pltpu.VMEM((6, pairs, rows, LANES), F32),
        ],
        compiler_params=PARAMS,
        cost_estimate=cost(2 * 10**10),
        name="pair_flows",
    )(notlast, fwd_offset, after, after_low, after_high, along, down, form_rows, form_cols,
      own_patch, own_window, fwd_offset, bwd_offset, valid)


def body(image, fwd_offset, bwd_offset, valid):
    sec_dev, height, width = image.shape
    rows, count = valid.shape[1:]
    pairs = count // 2
    sec_size, tile_size = lax.axis_size("sec"), lax.axis_size("tile")
    sections = sec_dev * sec_size
    earlier = [(i, i - 1) for i in range(1, sec_size)]
    arriving = lax.ppermute(image[:1], "sec", earlier)
    up = [(i, i + 1) for i in range(tile_size - 1)]
    back = [(i + 1, i) for i in range(tile_size - 1)]
    low = lax.ppermute(image[:, -OFFMAX:], "tile", up)
    high = lax.ppermute(image[:, :OFFMAX], "tile", back)
    edges = lax.ppermute(jnp.concatenate([low[:1], high[:1]], 1), "sec", earlier)
    after = jnp.concatenate([image[1:], arriving], 0)
    after_low = jnp.concatenate([low[1:], edges[:, :OFFMAX]], 0)
    after_high = jnp.concatenate([high[1:], edges[:, OFFMAX:]], 0)

    own_patch = patch_spectra(image, rows, pairs)
    own_window = window_spectra(bwd_offset, image, low, high, rows, pairs)
    place = lax.axis_index("sec") * sec_dev
    notlast = (place + jnp.arange(sec_dev, dtype=jnp.int32) < sections - 1).astype(jnp.int32)
    pair_flow, tiles = pair_flows(
        sec_size * tile_size, notlast, fwd_offset, after, after_low, after_high, own_patch, own_window, bwd_offset, valid
    )
    everywhere = lax.all_to_all(tiles, ("sec", "tile"), 0, 0)
    everywhere = (
        everywhere.reshape(sec_size, tile_size, sec_dev, 2, LANES)
        .transpose(0, 2, 1, 3, 4)
        .reshape(sections * tile_size, 2, LANES)
    )
    where = (place * tile_size + lax.axis_index("tile")).astype(jnp.int32).reshape(1)
    mesh_shift = pl.pallas_call(
        functools.partial(mesh_kernel, tile_size),
        out_shape=jax.ShapeDtypeStruct(pair_flow.shape, F32),
        in_specs=[SCALARS, pl.BlockSpec(memory_space=pltpu.VMEM)],
        out_specs=pl.BlockSpec(memory_space=pltpu.VMEM),
        compiler_params=pltpu.CompilerParams(vmem_limit_bytes=8 * 1024 * 1024),
        name="relax",
    )(where, everywhere)
    return pair_flow, mesh_shift


def solution(mesh):
    return jax.shard_map(
        body,
        mesh=mesh,
        in_specs=(
            P("sec", "tile", None),
            P("sec", None, "tile", None),
            P("sec", None, "tile", None),
            P("sec", "tile", None),
        ),
        out_specs=(P("sec", None, "tile", None), P("sec", None, "tile", None)),
        check_vma=False,
    )
```

```python
import functools

import jax
import jax.numpy as jnp
import ml_dtypes
import numpy as np
from jax import lax
from jax.experimental import pallas as pl
from jax.experimental.pallas import tpu as pltpu
from jax.sharding import PartitionSpec as P

PATCH = 128
HALF = PATCH // 2
OFFMAX = 16
ITERS = 3
LANES = 128
BF = jnp.bfloat16
F32 = jnp.float32


def split_table(table):
    high = table.astype(np.float32).astype(ml_dtypes.bfloat16)
    low = (table - high.astype(np.float64)).astype(np.float32).astype(ml_dtypes.bfloat16)
    return high, low


@functools.cache
def tables():
    place = np.arange(PATCH)
    quarter = np.sin(np.arange(PATCH // 4 + 1) * (2 * np.pi / PATCH))
    sine = np.concatenate([quarter, quarter[-2::-1], -quarter[1:], -quarter[-2:0:-1]])
    cosine = np.roll(sine, -PATCH // 4)
    basis = np.zeros((PATCH, PATCH))
    basis[0] = place % 2 == 0
    basis[HALF] = place % 2 == 1
    for u in range(1, HALF):
        basis[u] = cosine[(u * place) % PATCH]
        basis[HALF + u] = sine[(u * place) % PATCH]
    lag = ((place + HALF) % PATCH) - HALF
    full = (basis * lag) @ basis.T
    form = np.zeros((HALF, PATCH))
    form[1:] = 2 * full[HALF + 1 :]
    form[1:, HALF + 1 :] = 0
    form[0, :HALF] = basis[:HALF, HALF]
    basis_high, basis_low = split_table(basis)
    form_high, form_low = split_table(form)

    def side_by_side(part):
        out = np.zeros((2 * PATCH, 2 * PATCH), ml_dtypes.bfloat16)
        for t in range(2):
            for s in range(2):
                out[t * PATCH : (t + 1) * PATCH, s * PATCH + t * HALF : s * PATCH + (t + 1) * HALF] = (
                    part[s * HALF : (s + 1) * HALF].T
                )
        return out

    def columns(part):
        out = np.zeros((2 * PATCH, PATCH), ml_dtypes.bfloat16)
        for t in range(2):
            for s in range(2):
                out[s * PATCH + t * HALF : s * PATCH + (t + 1) * HALF, t * HALF : (t + 1) * HALF] = (
                    part[:, s * HALF : (s + 1) * HALF].T
                )
        return out

    along = np.concatenate([side_by_side(basis_high), side_by_side(basis_low)], 0)
    down = np.concatenate(
        [np.concatenate([basis_high, basis_high], 1), np.concatenate([basis_low, basis_low * 0], 1)], 0
    )
    form_rows = np.concatenate(
        [np.concatenate([form_high, form_high], 1), np.concatenate([form_low, form_low * 0], 1)], 0
    )
    form_cols = np.concatenate([columns(form_high), columns(form_low)], 1)
    return along, down, form_rows, form_cols


def dot(a, b):
    return jnp.dot(a, b, preferred_element_type=F32)


def split(x):
    high = x.astype(BF)
    return high, (x - high.astype(F32)).astype(BF)


def fill_padded(padded, image_ref, low_ref, high_ref):
    rows, cols = image_ref.shape
    padded[:, 0:LANES] = jnp.zeros((padded.shape[0], LANES), F32)
    padded[:, LANES + cols :] = jnp.zeros((padded.shape[0], LANES), F32)
    padded[2 * OFFMAX + rows :, :] = jnp.zeros((8, padded.shape[1]), F32)
    padded[0:OFFMAX, LANES : LANES + cols] = low_ref[...].astype(F32)
    padded[OFFMAX + rows : 2 * OFFMAX + rows, LANES : LANES + cols] = high_ref[...].astype(F32)

    def step(i, carry):
        r = pl.multiple_of(i * 64, 64)
        padded[pl.ds(r + OFFMAX, 64), LANES : LANES + cols] = image_ref[pl.ds(r, 64), :].astype(F32)
        return carry

    lax.fori_loop(0, rows // 64, step, 0)


def fill_window_row(window, padded, off_ref, s, c, i):
    lane = lax.broadcasted_iota(jnp.int32, (PATCH + 8, LANES), 1)
    deep = lax.broadcasted_iota(jnp.int32, (PATCH // 8, 8, LANES), 1)
    for t in range(2):
        j = 2 * c + t
        top = OFFMAX + off_ref[s, 0, i, j]
        ox = off_ref[s, 1, i, j]
        left = (ox < 0).astype(jnp.int32)
        base = pl.multiple_of((j + 1 - left) * LANES, LANES)
        shift = ox + LANES * left
        aligned = pl.multiple_of(i * PATCH + jnp.bitwise_and(top, -8), 8)
        block = padded[pl.ds(aligned, PATCH + 8), pl.ds(base, 2 * LANES)]
        turn = jnp.bitwise_and(LANES - shift, LANES - 1)
        first = pltpu.roll(block[:, :LANES], turn, 1)
        second = pltpu.roll(block[:, LANES:], turn, 1)
        cut = jnp.where(lane < LANES - shift, first, second)
        over = jnp.bitwise_and(top, 7)
        cut = pltpu.roll(cut.reshape(PATCH // 8 + 1, 8, LANES), jnp.bitwise_and(8 - over, 7), 1)
        cut = jnp.where(deep < 8 - over, cut[:-1], cut[1:]).reshape(PATCH, LANES)
        window[i * PATCH : (i + 1) * PATCH, t * LANES : (t + 1) * LANES] = cut.astype(BF)


def first_stage(block, along_ref, parts):
    high, low = split(dot(jnp.concatenate([block, block], 1), along_ref[...]))
    rows = parts.shape[0]
    parts[:, :PATCH] = high.reshape(rows, PATCH, 2 * PATCH)
    parts[:, PATCH:] = low.reshape(rows, PATCH, 2 * PATCH)


def second_stage(part, down_ref):
    both = dot(down_ref[...], part)
    return both[:PATCH] + both[PATCH:]


def store_coefficients(out_ref, coef):
    row = lax.broadcasted_iota(jnp.int32, (8, LANES), 0)
    lane = lax.broadcasted_iota(jnp.int32, (8, LANES), 1)
    corner = jnp.logical_and(row == 0, lane % HALF == 0)
    out_ref[...] = coef
    mean = 0.25 * (
        coef[0:8, :LANES] + coef[0:8, LANES:] + coef[HALF : HALF + 8, :LANES] + coef[HALF : HALF + 8, LANES:]
    )
    mean = jnp.where(corner, mean, 0.0)
    for r in (0, HALF):
        for q in (0, LANES):
            out_ref[r : r + 8, q : q + LANES] = coef[r : r + 8, q : q + LANES] - mean


def patch_kernel(image_ref, along_ref, down_ref, out_ref, parts):
    rows = image_ref.shape[0] // PATCH
    s, c = pl.program_id(0), pl.program_id(1)
    first_stage(image_ref[...], along_ref, parts)
    for i in range(rows):
        store_coefficients(out_ref.at[s, c, i], second_stage(parts[i], down_ref))


def window_kernel(off_ref, image_ref, low_ref, high_ref, along_ref, down_ref, out_ref, padded, window, parts):
    s, c = pl.program_id(0), pl.program_id(1)
    rows = image_ref.shape[0] // PATCH

    @pl.when(c == 0)
    def _():
        fill_padded(padded, image_ref, low_ref, high_ref)
        for i in range(rows):
            fill_window_row(window.at[0], padded, off_ref, s, 0, i)

    first_stage(window[c % 2], along_ref, parts)
    following = jnp.minimum(c + 1, pl.num_programs(1) - 1)
    for i in range(rows):
        store_coefficients(out_ref.at[s, c, i], second_stage(parts[i], down_ref))
        fill_window_row(window.at[(c + 1) % 2], padded, off_ref, s, following, i)


def cross(a_ref, b_ref, coef, pieces):
    lane = lax.broadcasted_iota(jnp.int32, (16, LANES), 1)
    row = lax.broadcasted_iota(jnp.int32, (16, LANES), 0)
    sign_j = jnp.where(lane % HALF == 0, -1.0, 1.0).astype(F32)
    first_row = jnp.where(row == 0, -1.0, 1.0).astype(F32)
    total = jnp.zeros((16, LANES), F32)
    for g in range(HALF // 16):
        top, bottom = slice(16 * g, 16 * g + 16), slice(HALF + 16 * g, HALF + 16 * g + 16)
        acc, acs, asc, ass = a_ref[top, :LANES], a_ref[top, LANES:], a_ref[bottom, :LANES], a_ref[bottom, LANES:]
        bcc, bcs, bsc, bss = b_ref[top, :LANES], b_ref[top, LANES:], b_ref[bottom, :LANES], b_ref[bottom, LANES:]
        acs_j, ass_j = acs * sign_j, ass * sign_j
        cc = acc * bcc + acs * bcs + asc * bsc + ass * bss
        cs = acc * bcs + asc * bss - (acs_j * bcc + ass_j * bsc)
        turned_sc = asc * bcc + ass * bcs
        turned_ss = asc * bcs - ass_j * bcc
        if g == 0:
            turned_sc, turned_ss = turned_sc * first_row, turned_ss * first_row
        sc = acc * bsc + acs * bss - turned_sc
        ss = acc * bss - acs_j * bsc - turned_ss
        total = total + (cc * cc + cs * cs + sc * sc + ss * ss)
        for where, lanes, value in (
            (top, slice(0, LANES), cc),
            (top, slice(LANES, 2 * LANES), cs),
            (bottom, slice(0, LANES), sc),
            (bottom, slice(LANES, 2 * LANES), ss),
        ):
            high, low = split(value)
            coef[where, lanes] = value
            pieces[where, lanes] = high
            pieces[slice(PATCH + where.start, PATCH + where.stop), lanes] = low
    return jnp.sum(total, axis=0, keepdims=True)


def moments(coef, pieces, rows_ref, cols_ref):
    down = dot(rows_ref[...], pieces[...])
    across = dot(pieces[...], cols_ref[...])
    down = down[:HALF] + down[HALF:]
    across = across[:PATCH, :LANES] + across[:PATCH, LANES:] + across[PATCH:, :LANES]
    row8 = lax.broadcasted_iota(jnp.int32, (8, 2 * LANES), 0)
    head = down[0:8]
    moment_r = jnp.where(row8 == 0, -float(HALF) * head, coef[HALF : HALF + 8, :]) * head
    for g in range(1, HALF // 8):
        moment_r = moment_r + down[8 * g : 8 * g + 8] * coef[HALF + 8 * g : HALF + 8 * g + 8, :]
    moment_r = moment_r[:, :LANES] + moment_r[:, LANES:]
    lane8 = lax.broadcasted_iota(jnp.int32, (8, LANES), 1) % HALF == 0
    moment_c = jnp.zeros((8, LANES), F32)
    for g in range(PATCH // 8):
        piece = across[8 * g : 8 * g + 8]
        other = jnp.where(lane8, -float(HALF) * piece, coef[8 * g : 8 * g + 8, LANES:])
        moment_c = moment_c + other * piece
    return jnp.sum(moment_r, axis=0, keepdims=True), jnp.sum(moment_c, axis=0, keepdims=True)


def pair_kernel(
    place_ref, off_ref, image_ref, low_ref, high_ref, along_ref, down_ref, rows_ref, cols_ref,
    own_patch, own_window, fwd_ref, bwd_ref, valid_ref, flow_out, tile_out,
    padded, window, parts, left, right, coef, pieces, sums,
):
    s = pl.program_id(0)
    rows = image_ref.shape[0] // PATCH
    pairs = own_patch.shape[1]
    steps = pairs * rows

    def first_image(c):
        first_stage(image_ref[:, 2 * c * LANES : 2 * (c + 1) * LANES], along_ref, parts.at[c % 2, 0])

    def first_window(c):
        first_stage(window[c % 2], along_ref, parts.at[c % 2, 1])

    def cut(c, i):
        fill_window_row(window.at[c % 2], padded, off_ref, s, c, i)

    def spectra(n):
        c, i = divmod(n, rows)
        store_coefficients(left.at[n % 2], second_stage(parts[c % 2, 0, i], down_ref))
        store_coefficients(right.at[n % 2], second_stage(parts[c % 2, 1, i], down_ref))

    def products(n):
        c, i = divmod(n, rows)
        k = n % 2
        sums[0, c, i : i + 1, :] = cross(own_patch.at[s, c, i], right.at[k], coef.at[0, k], pieces.at[0, k])
        sums[3, c, i : i + 1, :] = cross(left.at[k], own_window.at[s, c, i], coef.at[1, k], pieces.at[1, k])

    def centroid(n):
        c, i = divmod(n, rows)
        for d in range(2):
            by_row, by_col = moments(coef.at[d, n % 2], pieces.at[d, n % 2], rows_ref, cols_ref)
            sums[3 * d + 1, c, i : i + 1, :] = by_row
            sums[3 * d + 2, c, i : i + 1, :] = by_col

    fill_padded(padded, image_ref, low_ref, high_ref)
    first_image(0)
    for i in range(rows):
        cut(0, i)
    first_window(0)
    spectra(0)
    early = max(rows - 2, 1)
    ready = [i * rows // early for i in range(early + 1)]
    for n in range(steps):
        c, i = divmod(n, rows)
        if c + 1 < pairs and i < early:
            for r in range(ready[i], ready[i + 1]):
                cut(c + 1, r)
            if i == 1:
                first_image(c + 1)
            if i == early - 1:
                first_window(c + 1)
        if n + 1 < steps:
            spectra(n + 1)
        products(n)
        if n:
            centroid(n - 1)
    centroid(steps - 1)

    count = 2 * sums.shape[1]
    lane = lax.broadcasted_iota(jnp.int32, (rows, LANES), 1)
    gathered = []
    for k in range(6):
        value = jnp.zeros((rows, LANES), F32)
        for p in range(sums.shape[1]):
            held = sums[k, p]
            for t in range(2):
                mine = (lane >= HALF) if t else (lane < HALF)
                value = jnp.where(
                    lane == 2 * p + t, jnp.sum(jnp.where(mine, held, 0.0), axis=1, keepdims=True), value
                )
        gathered.append(value[:, :count])
    scale = (2.0 / PATCH) ** 4 * HALF * HALF
    lag_scale = scale / HALF
    eps = PATCH * PATCH * 1e-6
    notlast = place_ref[s].astype(F32)
    weight = valid_ref[...].astype(F32) * notlast
    flows = []
    for comp in range(2):
        fwd = gathered[1 + comp] * lag_scale / (gathered[0] * scale + eps) + fwd_ref[comp].astype(F32)
        bwd = gathered[4 + comp] * lag_scale / (gathered[3] * scale + eps) + bwd_ref[comp].astype(F32)
        flow = 0.5 * (fwd - bwd) * notlast
        flow_out[comp] = flow
        flows.append(flow)
    fill = jnp.zeros((rows, LANES - 4 * count), F32)
    wide = jnp.concatenate(flows + [weight, weight, fill], axis=1)
    row = lax.broadcasted_iota(jnp.int32, (rows, LANES), 0)
    group = 2 * count
    packed = []
    for begin in (0, group):
        line = jnp.zeros((rows, LANES), F32)
        for i in range(rows):
            turned = pltpu.roll(wide, (group * i - begin) % LANES, 1)
            line = jnp.where(jnp.logical_and(row == i, lane // group == i), turned, line)
        packed.append(jnp.sum(line, axis=0, keepdims=True))
    packed = jnp.concatenate(packed, axis=0)
    for k in range(tile_out.shape[0]):
        tile_out[k, s] = packed


def mesh_kernel(tiles, all_ref, shift_out):
    bands = all_ref.shape[0]
    sec_dev, _, rows, count = shift_out.shape
    group = 2 * count
    assert rows * group == LANES
    everything = all_ref[...]
    flow, weight = everything[:, 0], everything[:, 1]
    line = lax.broadcasted_iota(jnp.int32, (bands, LANES), 0)
    lane = lax.broadcasted_iota(jnp.int32, (bands, LANES), 1)
    band = line % tiles
    col, is_x, patch_row = lane % count, lane // count % 2, lane // group
    pulled = weight * flow

    def over_section(x):
        total = x
        for k in range(1, tiles):
            total = total + jnp.where(band >= k, pltpu.roll(x, k, 0), pltpu.roll(x, bands - tiles + k, 0))
        return total

    sum_y = jnp.sum(jnp.where(is_x == 0, pulled, 0.0), axis=1, keepdims=True)
    sum_x = jnp.sum(jnp.where(is_x == 1, pulled, 0.0), axis=1, keepdims=True)
    counts = jnp.sum(jnp.where(is_x == 0, weight, 0.0), axis=1, keepdims=True)
    sums = over_section(jnp.where(is_x == 0, sum_y, sum_x))
    mean = sums / jnp.maximum(over_section(jnp.broadcast_to(counts, sums.shape)), 1.0)
    shift = jnp.where(line >= tiles, pltpu.roll(mean, tiles, 0), 0.0)
    reach = tiles
    while reach < bands:
        shift = shift + jnp.where(line >= reach, pltpu.roll(shift, reach, 0), 0.0)
        reach *= 2
    at_top, at_bottom = patch_row == 0, patch_row == rows - 1
    one = lambda condition: condition.astype(F32)
    has_left, has_right = one(col > 0), one(col < count - 1)
    has_up = one(jnp.logical_or(band > 0, patch_row > 0))
    has_down = one(jnp.logical_or(band < tiles - 1, patch_row < rows - 1))
    degree = has_left + has_right + has_up + has_down
    not_first = one(line >= tiles)
    not_end = one(line < bands - tiles)
    weight_next, pulled_next = weight * not_end, pulled
    for _ in range(ITERS):
        lower, upper = pltpu.roll(shift, group, 1), pltpu.roll(shift, LANES - group, 1)
        above = jnp.where(at_top, pltpu.roll(lower, 1, 0), lower)
        below = jnp.where(at_bottom, pltpu.roll(upper, bands - 1, 0), upper)
        plane = (
            has_up * above
            + has_down * below
            + has_left * pltpu.roll(shift, 1, 1)
            + has_right * pltpu.roll(shift, LANES - 1, 1)
            - degree * shift
        )
        spring = weight_next * (pltpu.roll(shift, bands - tiles, 0) - shift) - pulled_next
        between = spring - not_first * pltpu.roll(spring, tiles, 0)
        shift = shift + 0.25 * (plane + between)
    mine_line = lax.broadcasted_iota(jnp.int32, (bands, LANES), 0)
    row = lax.broadcasted_iota(jnp.int32, (rows, LANES), 0)
    place = lax.axis_index("sec") * sec_dev * tiles + lax.axis_index("tile")
    for k in range(sec_dev):
        mine = jnp.sum(jnp.where(mine_line == place + k * tiles, shift, 0.0), axis=0, keepdims=True)
        spread = jnp.zeros((rows, LANES), F32)
        wide = jnp.broadcast_to(mine, (rows, LANES))
        for i in range(rows):
            spread = jnp.where(row == i, pltpu.roll(wide, (LANES - group * i) % LANES, 1), spread)
        shift_out[k, 0] = spread[:, :count]
        shift_out[k, 1] = spread[:, count:group]


def section_spec(shape):
    return pl.BlockSpec((None,) + shape[1:], lambda s, *_: (s,) + (0,) * (len(shape) - 1))


def whole_spec(shape):
    return pl.BlockSpec(shape, lambda *_: (0,) * len(shape))


SCALARS = pl.BlockSpec(memory_space=pltpu.SMEM)


PARAMS = pltpu.CompilerParams(vmem_limit_bytes=24 * 1024 * 1024)


def in_hbm(array):
    return pltpu.with_memory_space_constraint(array, pltpu.HBM)


def cost(flops):
    return pl.CostEstimate(flops=flops, bytes_accessed=10**7, transcendentals=0)


def coef_layout(sec_dev, rows, pairs):
    return pltpu.VMEM((sec_dev, pairs, rows, PATCH, 2 * PATCH), F32), pl.BlockSpec(memory_space=pltpu.VMEM)


def patch_spectra(image, rows, pairs):
    sec_dev, height, width = image.shape
    along, down, _, _ = (jnp.asarray(t) for t in tables())
    shape, spec = coef_layout(sec_dev, rows, pairs)
    return pl.pallas_call(
        patch_kernel,
        grid=(sec_dev, pairs),
        out_shape=shape,
        in_specs=[
            pl.BlockSpec((None, height, 2 * LANES), lambda s, c: (s, 0, c)),
            whole_spec(along.shape),
            whole_spec(down.shape),
        ],
        out_specs=spec,
        scratch_shapes=[pltpu.VMEM((rows, 2 * PATCH, 2 * PATCH), BF)],
        compiler_params=PARAMS,
        cost_estimate=cost(5 * 10**9),
        name="patch_spectra",
    )(*(in_hbm(x) for x in (image, along, down)))


def window_spectra(offset, image, low, high, rows, pairs):
    sec_dev, height, width = image.shape
    along, down, _, _ = (jnp.asarray(t) for t in tables())
    shape, spec = coef_layout(sec_dev, rows, pairs)
    return pl.pallas_call(
        window_kernel,
        grid=(sec_dev, pairs),
        out_shape=shape,
        in_specs=[
            SCALARS,
            section_spec(image.shape),
            section_spec(low.shape),
            section_spec(high.shape),
            whole_spec(along.shape),
            whole_spec(down.shape),
        ],
        out_specs=spec,
        scratch_shapes=[
            pltpu.VMEM((height + 2 * OFFMAX + 8, width + 2 * LANES), F32),
            pltpu.VMEM((2, height, 2 * LANES), BF),
            pltpu.VMEM((rows, 2 * PATCH, 2 * PATCH), BF),
        ],
        compiler_params=PARAMS,
        cost_estimate=cost(5 * 10**9),
        name="window_spectra",
    )(offset, image, low, high, along, down)


def pair_flows(devices, notlast, fwd_offset, after, after_low, after_high, own_patch, own_window, bwd_offset, valid):
    sec_dev, height, width = after.shape
    rows, count = valid.shape[1:]
    pairs = count // 2
    along, down, form_rows, form_cols = (jnp.asarray(t) for t in tables())
    _, coef_spec = coef_layout(sec_dev, rows, pairs)
    flow_shape = jax.ShapeDtypeStruct((sec_dev, 2, rows, count), F32)
    return pl.pallas_call(
        pair_kernel,
        grid=(sec_dev,),
        out_shape=(flow_shape, jax.ShapeDtypeStruct((devices, sec_dev, 2, LANES), F32)),
        in_specs=[
            SCALARS,
            SCALARS,
            section_spec(after.shape),
            section_spec(after_low.shape),
            section_spec(after_high.shape),
            whole_spec(along.shape),
            whole_spec(down.shape),
            whole_spec(form_rows.shape),
            whole_spec(form_cols.shape),
            coef_spec,
            coef_spec,
            section_spec(fwd_offset.shape),
            section_spec(bwd_offset.shape),
            section_spec(valid.shape),
        ],
        out_specs=(section_spec(flow_shape.shape), pl.BlockSpec(memory_space=pltpu.VMEM)),
        scratch_shapes=[
            pltpu.VMEM((height + 2 * OFFMAX + 8, width + 2 * LANES), F32),
            pltpu.VMEM((2, height, 2 * LANES), BF),
            pltpu.VMEM((2, 2, rows, 2 * PATCH, 2 * PATCH), BF),
            pltpu.VMEM((2, PATCH, 2 * PATCH), F32),
            pltpu.VMEM((2, PATCH, 2 * PATCH), F32),
            pltpu.VMEM((2, 2, PATCH, 2 * PATCH), F32),
            pltpu.VMEM((2, 2, 2 * PATCH, 2 * PATCH), BF),
            pltpu.VMEM((6, pairs, rows, LANES), F32),
        ],
        compiler_params=PARAMS,
        cost_estimate=cost(2 * 10**10),
        name="pair_flows",
    )(notlast, fwd_offset, after, after_low, after_high, along, down, form_rows, form_cols,
      own_patch, own_window, fwd_offset, bwd_offset, valid)


def body(image, fwd_offset, bwd_offset, valid):
    sec_dev, height, width = image.shape
    rows, count = valid.shape[1:]
    pairs = count // 2
    sec_size, tile_size = lax.axis_size("sec"), lax.axis_size("tile")
    sections = sec_dev * sec_size
    earlier = [(i, i - 1) for i in range(1, sec_size)]
    arriving = lax.ppermute(image[:1], "sec", earlier)
    up = [(i, i + 1) for i in range(tile_size - 1)]
    back = [(i + 1, i) for i in range(tile_size - 1)]
    low = lax.ppermute(image[:, -OFFMAX:], "tile", up)
    high = lax.ppermute(image[:, :OFFMAX], "tile", back)
    edges = lax.ppermute(jnp.concatenate([low[:1], high[:1]], 1), "sec", earlier)
    after = jnp.concatenate([image[1:], arriving], 0)
    after_low = jnp.concatenate([low[1:], edges[:, :OFFMAX]], 0)
    after_high = jnp.concatenate([high[1:], edges[:, OFFMAX:]], 0)

    own_patch = patch_spectra(image, rows, pairs)
    own_window = window_spectra(bwd_offset, image, low, high, rows, pairs)
    place = lax.axis_index("sec") * sec_dev
    notlast = (place + jnp.arange(sec_dev, dtype=jnp.int32) < sections - 1).astype(jnp.int32)
    pair_flow, tiles = pair_flows(
        sec_size * tile_size, notlast, fwd_offset, after, after_low, after_high, own_patch, own_window, bwd_offset, valid
    )
    everywhere = lax.all_to_all(tiles, ("sec", "tile"), 0, 0)
    everywhere = (
        everywhere.reshape(sec_size, tile_size, sec_dev, 2, LANES)
        .transpose(0, 2, 1, 3, 4)
        .reshape(sections * tile_size, 2, LANES)
    )
    mesh_shift = pl.pallas_call(
        functools.partial(mesh_kernel, tile_size),
        out_shape=jax.ShapeDtypeStruct(pair_flow.shape, F32),
        in_specs=[pl.BlockSpec(memory_space=pltpu.VMEM)],
        out_specs=pl.BlockSpec(memory_space=pltpu.VMEM),
        compiler_params=pltpu.CompilerParams(vmem_limit_bytes=8 * 1024 * 1024),
        name="relax",
    )(everywhere)
    return pair_flow, mesh_shift


def solution(mesh):
    return jax.shard_map(
        body,
        mesh=mesh,
        in_specs=(
            P("sec", "tile", None),
            P("sec", None, "tile", None),
            P("sec", None, "tile", None),
            P("sec", "tile", None),
        ),
        out_specs=(P("sec", None, "tile", None), P("sec", None, "tile", None)),
        check_vma=False,
    )
```
